256 devices in a mesh: line: 32 (over z, y), block: 8 (over x, core).
Axes of the slice: x: 4, y: 4, z: 8, core: 2. Of those that a mesh axis runs over, the one named last changes fastest.
Arguments:
- estimate: bfloat16 [16, 32, 384, 2048], P('block', 'line'), may hold values from -6 to 6
- observed: bfloat16 [32, 384, 16384], P('line', None, 'block'), may hold values from -9 to 9
- offsets: int32 [16], P('block'), may hold values from 0 to 2047
- counts: int32 [8], P('block'), may hold values from 1 to 2, as said below
- coherence: float32 [32, 384], replicated, may hold values from 0.1 to 1
Outputs:
- updated: bfloat16 [16, 32, 384, 2048], P('block', 'line')
The draws below stay inside these ranges and needn't reach their ends.
Inputs may be any that keep to these rules, and one draw needn't show every extreme that they name: `counts`: in every draw some record block has exactly 2 shots.
All inputs are finite; a program needn't handle non-finite values.
Results may differ from the reference program's by a relative error of at most 0.012.
Values may be sent and summed in bfloat16 or wider, within the bound.
No kernel may reach another device: no remote copies, remote signals or barrier semaphores. Data moves between devices by JAX's collectives and lax.ppermute only.
A program may use at most 128 MiB of HBM per device.

```python
import math
import jax
import jax.numpy as jnp
from jax import lax

C = 384
TS = 2048
CAP = 2
NL = 32
BLOCKS = 8
SLOTS = 16
RECORD = 16384


def draw_counts(key, part):
    key = jax.random.fold_in(key, 11)
    first, second = jax.random.split(key)
    drawn = jax.random.randint(first, (BLOCKS,), 1, CAP + 1)
    chosen = jax.random.randint(second, (), 0, BLOCKS)
    return jnp.where(jnp.arange(BLOCKS) == chosen, CAP, drawn).astype(jnp.int32)


def set_ends(values, key, smallest, top_value):
    longest = values.shape.index(max(values.shape))
    spots = []
    for shift in (0, 1):
        where = [jax.random.randint(jax.random.fold_in(key, axis), (), 0, length) for axis, length in enumerate(values.shape)]
        where[longest] = (where[longest] + shift) % values.shape[longest]
        spots.append(tuple(where))
    return values.at[spots[0]].set(smallest).at[spots[1]].set(top_value)


def steps_of(rng, extent, pieces, least, top_value):
    def one(axis_at, blocks):
        heights = jax.random.uniform(jax.random.fold_in(jax.random.fold_in(rng, 6), axis_at), (blocks,), jnp.float32, least / len(pieces), top_value / len(pieces))
        return jnp.repeat(jnp.exp(heights), extent[axis_at] // blocks).reshape((-1,) + (1,) * (len(extent) - axis_at - 1))

    level = one(*pieces[0])
    for cut in pieces[1:]:
        level = level * one(*cut)
    return level


def bell_draw(own_key, extent, spread, reach, cuts=(), kind=jnp.bfloat16):
    loudness = steps_of(own_key, extent, cuts, -0.22, 0.18) if cuts else 1.0
    entries = jax.random.normal(own_key, extent, jnp.float32) * spread * loudness
    return jnp.minimum(jnp.maximum(entries, -reach), reach).astype(kind)


def setup_inputs(seed: int = 0) -> dict:
    arg_keys = jax.random.split(jax.random.key(seed), 6)
    return {
        "estimate": bell_draw(arg_keys[0], (SLOTS, NL, C, TS), 1.0, 6.0, ((0, 8), (1, 32))),
        "observed": bell_draw(arg_keys[1], (NL, C, RECORD), 1.5, 9.0, ((0, 32), (2, 8))),
        "offsets": set_ends(jax.random.randint(arg_keys[2], (SLOTS,), 0, TS), jax.random.fold_in(arg_keys[2], 1), 0, TS - 1).astype(jnp.int32),
        "counts": draw_counts(jax.random.fold_in(arg_keys[5], 71), 0),
        "coherence": jnp.clip(jax.random.uniform(arg_keys[4], (NL, C), jnp.float32, 0.1, 1.0), 0.1, 1.0),
    }


def tables(count):
    position = jnp.arange(count, dtype=jnp.int32)
    product = (position[:, None] * position[None, :]) % count
    angle = product.astype(jnp.float32) * (2.0 * math.pi / count)
    return jnp.cos(angle).astype(jnp.bfloat16), jnp.sin(angle).astype(jnp.bfloat16)


def widen(value):
    return value.astype(jnp.float32)


def filter_shot(pseudo, coherence):
    cos_inline, sin_inline = tables(C)
    cos_cross, sin_cross = tables(NL)
    spec_re = jnp.einsum("qc,lct->lqt", widen(cos_inline), widen(pseudo)).astype(jnp.bfloat16)
    spec_im = (-jnp.einsum("qc,lct->lqt", widen(sin_inline), widen(pseudo))).astype(jnp.bfloat16)
    cross_re = jnp.einsum("kl,lqt->kqt", widen(cos_cross), widen(spec_re)) + jnp.einsum("kl,lqt->kqt", widen(sin_cross), widen(spec_im))
    cross_im = jnp.einsum("kl,lqt->kqt", widen(cos_cross), widen(spec_im)) - jnp.einsum("kl,lqt->kqt", widen(sin_cross), widen(spec_re))
    weighted_re = (cross_re * coherence[:, :, None]).astype(jnp.bfloat16)
    weighted_im = (cross_im * coherence[:, :, None]).astype(jnp.bfloat16)
    back_re = (jnp.einsum("kl,kqt->lqt", widen(cos_cross), widen(weighted_re)) - jnp.einsum("kl,kqt->lqt", widen(sin_cross), widen(weighted_im))).astype(jnp.bfloat16)
    back_im = (jnp.einsum("kl,kqt->lqt", widen(cos_cross), widen(weighted_im)) + jnp.einsum("kl,kqt->lqt", widen(sin_cross), widen(weighted_re))).astype(jnp.bfloat16)
    total = jnp.einsum("qc,lqt->lct", widen(cos_inline), widen(back_re)) - jnp.einsum("qc,lqt->lct", widen(sin_inline), widen(back_im))
    return (total * (1.0 / (NL * C))).astype(jnp.bfloat16)


def reference(estimate, observed, offsets, counts, coherence):
    def slot_info(slot):
        owner = slot // CAP
        within = slot % CAP
        live = (within < counts[owner]).astype(jnp.float32)
        start = (owner * TS + offsets[slot]).astype(jnp.int32)
        return live, start

    def add_shot(slot, record):
        live, start = slot_info(slot)
        current = lax.dynamic_slice_in_dim(record, start, TS, 2)
        return lax.dynamic_update_slice_in_dim(record, current + widen(estimate[slot]) * live, start, 2)

    record = jnp.zeros((NL, C, RECORD + TS), jnp.float32)
    record = lax.fori_loop(0, SLOTS, add_shot, record)
    residual = (widen(observed) - record[:, :, :RECORD]).astype(jnp.bfloat16)
    extended = jnp.concatenate([residual, jnp.zeros((NL, C, TS), jnp.bfloat16)], axis=2)

    def one_slot(slot):
        live, start = slot_info(slot)
        pseudo = lax.dynamic_slice_in_dim(extended, start, TS, 2) * live.astype(jnp.bfloat16)
        filtered = filter_shot(pseudo, coherence)
        return ((widen(estimate[slot]) + widen(filtered)) * live).astype(jnp.bfloat16)

    return lax.map(one_slot, jnp.arange(SLOTS, dtype=jnp.int32))
```

```python
import functools
import math

import jax
import jax.numpy as jnp
from jax import lax
from jax.experimental import pallas as pl
from jax.experimental.pallas import tpu as pltpu
from jax.sharding import PartitionSpec as P

CHUNKS = 2
TILE = 256
LANES = 128
GROUP = 8
VMEM = 48 * 1024 * 1024


def passed_along(shard, axis, by):
    peers = lax.axis_size(axis)
    pairs = [(i, i + by) for i in range(peers) if 0 <= i + by < peers]
    return lax.ppermute(shard, axis, pairs)


def tables(count):
    position = jnp.arange(count, dtype=jnp.int32)
    product = position[:, None] * position[None, :] % count
    angle = product.astype(jnp.float32) * (2.0 * math.pi / count)
    return (jnp.cos(angle).astype(jnp.bfloat16), jnp.sin(angle).astype(jnp.bfloat16))


def rows_by_rows(left, right):
    return lax.dot_general(
        left, right, (((1,), (1,)), ((), ())), preferred_element_type=jnp.float32
    )


def blend_kernel(offsets, counts, estimate, observed, rest, tail):
    slots, width, length = estimate.shape
    tile = rest.shape[0]
    blocks = length // LANES
    window = tile // LANES + 1
    first = pl.program_id(0) * tile
    row = lax.broadcasted_iota(jnp.int32, (tile, window * LANES), 0)
    column = lax.broadcasted_iota(jnp.int32, (tile, window * LANES), 1)
    time = first + lax.broadcasted_iota(jnp.int32, (tile, width), 0)
    unit = (row == column)[:, :tile].astype(jnp.float32).astype(jnp.bfloat16)
    ahead = rows_by_rows(unit, observed[...])
    behind = jnp.zeros((tile, width), jnp.float32)
    for slot in range(slots):
        offset = offsets[slot]
        base = lax.rem(first - offset + length, length)
        begin = base // LANES
        part = base - begin * LANES
        pieces = [
            estimate[slot, :, pl.ds(pl.multiple_of(lax.rem(begin + j, blocks) * LANES, LANES), LANES)]
            for j in range(window)
        ]
        value = jnp.where(slot < counts[0], 1.0, 0.0).astype(jnp.float32)
        chosen = jnp.where(column == row + part, value, 0.0).astype(jnp.bfloat16)
        moved = rows_by_rows(chosen, jnp.concatenate(pieces, axis=1))
        here = time >= offset
        ahead = ahead - jnp.where(here, moved, 0.0)
        behind = behind + jnp.where(here, 0.0, moved)
    rest[...] = ahead
    tail[...] = behind.astype(jnp.bfloat16)


def blend(estimate, observed, offsets, counts):
    slots, width, length = estimate.shape
    return pl.pallas_call(
        blend_kernel,
        grid_spec=pltpu.PrefetchScalarGridSpec(
            num_scalar_prefetch=2,
            grid=(length // TILE,),
            in_specs=[
                pl.BlockSpec((slots, width, length), lambda i, *_: (0, 0, 0)),
                pl.BlockSpec((width, TILE), lambda i, *_: (0, i)),
            ],
            out_specs=[
                pl.BlockSpec((TILE, width), lambda i, *_: (i, 0)),
                pl.BlockSpec((TILE, width), lambda i, *_: (i, 0)),
            ],
        ),
        out_shape=[
            jax.ShapeDtypeStruct((length, width), jnp.float32),
            jax.ShapeDtypeStruct((length, width), jnp.bfloat16),
        ],
        compiler_params=pltpu.CompilerParams(vmem_limit_bytes=VMEM),
        name="blend",
    )(offsets, counts, estimate, observed)


def filter_kernel(scale, x, inward, ahead_cos, ahead_sin, behind, first, second, outward, y):
    lines, steps, width = x.shape
    half = inward.shape[1] // 2
    rows = lines * GROUP
    spec = jnp.dot(
        x[...].reshape(lines * steps, width), inward[...], preferred_element_type=jnp.float32
    ).reshape(lines, steps, 2 * half)
    results = []
    for at in range(0, steps, GROUP):
        part = spec[:, at : at + GROUP, :].reshape(rows, 2 * half).astype(jnp.bfloat16)
        re, im = part[:, :half], part[:, half:]
        cos_both = jnp.dot(ahead_cos[...], part, preferred_element_type=jnp.float32)
        sin_both = jnp.dot(ahead_sin[...], part, preferred_element_type=jnp.float32)
        w1, w2 = first[...], second[...]
        weighted_re = w1 * cos_both[:, :half] + w2 * sin_both[:, half:]
        weighted_im = w2 * cos_both[:, half:] - w1 * sin_both[:, :half]
        weighted = jnp.concatenate([weighted_re, weighted_im], axis=0).astype(jnp.bfloat16)
        back = jnp.dot(behind[...], weighted, preferred_element_type=jnp.float32)
        back = jnp.concatenate([back[:rows], back[rows:]], axis=1).astype(jnp.bfloat16)
        total = jnp.dot(back, outward[...], preferred_element_type=jnp.float32) * scale
        results.append(total.reshape(lines, GROUP, width))
    y[...] = jnp.concatenate(results, axis=1).astype(jnp.bfloat16)


def filter_tables(coherence):
    lines, width = coherence.shape
    half = width // 2
    padded = -(-half // LANES) * LANES
    cos_inline, sin_inline = tables(width)
    cos_cross, sin_cross = tables(lines)
    opposite = jnp.roll(coherence[::-1, ::-1], (1, 1), (0, 1))
    weight = 0.5 * (coherence + opposite)
    lowest = jnp.arange(half)[None, :] == 0
    first = weight[:, :half]
    second = jnp.where(lowest, weight[:, half : half + 1], first)

    def pad(value):
        return jnp.pad(value, ((0, 0), (0, padded - half)))

    def spread(value):
        return jnp.repeat(pad(value), GROUP, axis=0)

    cos_half = cos_inline[:, :half]
    im_half = jnp.where(lowest, cos_inline[:, half : half + 1], -sin_inline[:, :half])
    inward = jnp.concatenate([pad(cos_half), pad(im_half)], axis=1)
    double = jnp.where(lowest, 1.0, 2.0).astype(jnp.bfloat16)
    outward = jnp.concatenate([pad(cos_half * double), pad(im_half * double)], axis=1).T
    unit = jnp.eye(GROUP, dtype=jnp.bfloat16)
    cos_wide = jnp.kron(cos_cross, unit)
    sin_wide = jnp.kron(sin_cross, unit)
    behind = jnp.concatenate(
        [
            jnp.concatenate([cos_wide, -sin_wide], axis=1),
            jnp.concatenate([sin_wide, cos_wide], axis=1),
        ],
        axis=0,
    )
    return (inward, cos_wide, sin_wide, behind, spread(first), spread(second), outward)


def filtered(x, prepared, lines):
    width = x.shape[1]
    steps = x.shape[0] // lines
    scale = 1.0 / (lines * width)
    tall = 2 * GROUP
    held = [
        pl.BlockSpec(value.shape, lambda i, r=value.ndim: (0,) * r) for value in prepared
    ]
    out = pl.pallas_call(
        functools.partial(filter_kernel, scale),
        grid=(steps // tall,),
        in_specs=[pl.BlockSpec((lines, tall, width), lambda i: (0, i, 0))] + held,
        out_specs=pl.BlockSpec((lines, tall, width), lambda i: (0, i, 0)),
        out_shape=jax.ShapeDtypeStruct((lines, steps, width), jnp.bfloat16),
        compiler_params=pltpu.CompilerParams(vmem_limit_bytes=VMEM),
        cost_estimate=pl.CostEstimate(
            flops=steps * 120_000_000, bytes_accessed=4 * x.size, transcendentals=0
        ),
        name="filter",
    )(x.reshape(lines, steps, width), *prepared)
    return out.reshape(lines * steps, width)


def update_kernel(chunks, offsets, counts, estimate, *refs):
    sources = refs[: 2 * chunks]
    out, turned = refs[2 * chunks :]
    slots, width, tile = estimate.shape
    piece = sources[0].shape[0]
    window = (tile // LANES + 1) * LANES

    @pl.when(pl.program_id(0) == 0)
    def _():
        unit = (
            lax.broadcasted_iota(jnp.int32, (width, width), 0)
            == lax.broadcasted_iota(jnp.int32, (width, width), 1)
        ).astype(jnp.float32).astype(jnp.bfloat16)
        for index, source in enumerate(sources):
            for at in range(0, piece, TILE):
                turned[:, pl.ds(index * piece + at, TILE)] = rows_by_rows(
                    unit, source[pl.ds(at, TILE), :]
                ).astype(jnp.bfloat16)
        turned[:, pl.ds(2 * chunks * piece, LANES)] = jnp.zeros((width, LANES), jnp.bfloat16)

    row = lax.broadcasted_iota(jnp.int32, (window, tile), 0)
    column = lax.broadcasted_iota(jnp.int32, (window, tile), 1)
    for slot in range(slots):
        base = offsets[slot] + pl.program_id(0) * tile
        begin = base // LANES
        part = base - begin * LANES
        chosen = (row == column + part).astype(jnp.float32).astype(jnp.bfloat16)
        taken = turned[:, pl.ds(pl.multiple_of(begin * LANES, LANES), window)]
        moved = jnp.dot(taken, chosen, preferred_element_type=jnp.float32)
        total = estimate[slot].astype(jnp.float32) + moved
        out[slot] = jnp.where(slot < counts[0], total, 0.0).astype(jnp.bfloat16)


def update(estimate, own, following, offsets, counts):
    slots, width, length = estimate.shape
    chunks = len(own)
    piece = length // chunks
    spec = pl.BlockSpec((slots, width, TILE), lambda i, *_: (0, 0, i))
    whole = pl.BlockSpec((piece, width), lambda i, *_: (0, 0))
    return pl.pallas_call(
        functools.partial(update_kernel, chunks),
        grid_spec=pltpu.PrefetchScalarGridSpec(
            num_scalar_prefetch=2,
            grid=(length // TILE,),
            in_specs=[spec] + [whole] * (2 * chunks),
            out_specs=spec,
            scratch_shapes=[pltpu.VMEM((width, 2 * length + LANES), jnp.bfloat16)],
        ),
        out_shape=jax.ShapeDtypeStruct((slots, width, length), jnp.bfloat16),
        compiler_params=pltpu.CompilerParams(vmem_limit_bytes=VMEM),
        name="update",
    )(offsets, counts, estimate, *own, *following)


def body(estimate, observed, offsets, counts, coherence):
    slots, _, width, length = estimate.shape
    lines = lax.axis_size("line")
    estimate = estimate.reshape(slots, width, length)
    observed = observed.reshape(width, length)
    rest, tail = blend(estimate, observed, offsets, counts)
    prepared = filter_tables(coherence)
    piece = length // CHUNKS
    spread = []
    for chunk in range(CHUNKS):
        part = slice(chunk * piece, (chunk + 1) * piece)
        incoming = passed_along(tail[part], "block", 1)
        residual = (rest[part] - incoming.astype(jnp.float32)).astype(jnp.bfloat16)
        spread.append(lax.all_to_all(residual, "line", split_axis=0, concat_axis=0, tiled=True))
    own, following = [], []
    for chunk in range(CHUNKS):
        back = filtered(spread[chunk], prepared, lines)
        back = lax.all_to_all(back, "line", split_axis=0, concat_axis=0, tiled=True)
        own.append(back)
        following.append(passed_along(back, "block", -1))
    updated = update(estimate, own, following, offsets, counts)
    return updated.reshape(slots, 1, width, length)


def solution(mesh):
    return jax.shard_map(
        body,
        mesh=mesh,
        in_specs=(
            P("block", "line", None, None),
            P("line", None, "block"),
            P("block"),
            P("block"),
            P(),
        ),
        out_specs=P("block", "line", None, None),
        check_vma=False,
    )
```

```python
import functools
import math

import jax
import jax.numpy as jnp
import ml_dtypes
import numpy as np
from jax import lax
from jax.experimental import pallas as pl
from jax.experimental.pallas import tpu as pltpu
from jax.sharding import PartitionSpec as P

CHUNKS = 2
TILE = 256
LANES = 128
GROUP = 8
TALL = 32
VMEM = 48 * 1024 * 1024


def tables(count):
    position = np.arange(count, dtype=np.int32)
    product = position[:, None] * position[None, :] % count
    angle = product.astype(np.float32) * np.float32(2.0 * math.pi / count)
    rounded = lambda value: value.astype(ml_dtypes.bfloat16).astype(np.float32)
    return (rounded(np.cos(angle)), rounded(np.sin(angle)))


def rows_by_rows(left, right):
    return lax.dot_general(
        left, right, (((1,), (1,)), ((), ())), preferred_element_type=jnp.float32
    )


def turned_shots(first, tile, offsets, counts, estimate):
    slots, width, length = estimate.shape
    blocks = length // LANES
    window = tile // LANES + 1
    row = lax.broadcasted_iota(jnp.int32, (tile, window * LANES), 0)
    column = lax.broadcasted_iota(jnp.int32, (tile, window * LANES), 1)
    time = first + lax.broadcasted_iota(jnp.int32, (tile, width), 0)
    for slot in range(slots):
        offset = offsets[slot]
        base = lax.rem(first - offset + length, length)
        begin = base // LANES
        part = base - begin * LANES
        pieces = [
            estimate[slot, :, pl.ds(pl.multiple_of(lax.rem(begin + j, blocks) * LANES, LANES), LANES)]
            for j in range(window)
        ]
        value = jnp.where(slot < counts[0], 1.0, 0.0).astype(jnp.float32)
        chosen = jnp.where(column == row + part, value, 0.0).astype(jnp.bfloat16)
        yield time >= offset, rows_by_rows(chosen, jnp.concatenate(pieces, axis=1))


def tail_kernel(offsets, counts, estimate, *tails):
    tile, width = tails[0].shape
    step = pl.program_id(0)
    per = pl.num_programs(0) // len(tails)
    behind = jnp.zeros((tile, width), jnp.float32)
    for here, moved in turned_shots(step * tile, tile, offsets, counts, estimate):
        behind = behind + jnp.where(here, 0.0, moved)
    for chunk, tail in enumerate(tails):

        @pl.when(step // per == chunk)
        def _(tail=tail):
            tail[...] = behind.astype(jnp.bfloat16)


def tails_of(estimate, offsets, counts):
    slots, width, length = estimate.shape
    piece = length // CHUNKS
    per = piece // TILE
    return pl.pallas_call(
        tail_kernel,
        grid_spec=pltpu.PrefetchScalarGridSpec(
            num_scalar_prefetch=2,
            grid=(length // TILE,),
            in_specs=[pl.BlockSpec((slots, width, length), lambda i, *_: (0, 0, 0))],
            out_specs=[
                pl.BlockSpec(
                    (TILE, width),
                    lambda i, *_, c=chunk: (jnp.clip(i - c * per, 0, per - 1), 0),
                )
                for chunk in range(CHUNKS)
            ],
        ),
        out_shape=[jax.ShapeDtypeStruct((piece, width), jnp.bfloat16)] * CHUNKS,
        compiler_params=pltpu.CompilerParams(vmem_limit_bytes=VMEM),
        cost_estimate=pl.CostEstimate(
            flops=3_000_000_000, bytes_accessed=5_000_000, transcendentals=0
        ),
        name="tails",
    )(offsets, counts, estimate)


def rest_kernel(begin_at, offsets, counts, odd, estimate, observed, *refs):
    *incoming, out = refs
    tile, width = out.shape
    first = begin_at + pl.program_id(0) * tile
    unit = (
        lax.broadcasted_iota(jnp.int32, (tile, tile), 0)
        == lax.broadcasted_iota(jnp.int32, (tile, tile), 1)
    ).astype(jnp.float32).astype(jnp.bfloat16)
    ahead = rows_by_rows(unit, observed[...])
    for here, moved in turned_shots(first, tile, offsets, counts, estimate):
        ahead = ahead - jnp.where(here, moved, 0.0)
    if incoming:
        swapped, crossed = (ref[...].astype(jnp.float32) for ref in incoming)
        ahead = ahead - jnp.where(odd[0] == 1, swapped, crossed)
    out[...] = ahead.astype(out.dtype)


def rest_of(estimate, observed, offsets, counts, odd, chunk, incoming, dtype, cost):
    slots, width, length = estimate.shape
    piece = length // CHUNKS
    tiles = piece // TILE
    rows = pl.BlockSpec((TILE, width), lambda i, *_: (i, 0))
    return pl.pallas_call(
        functools.partial(rest_kernel, chunk * piece),
        grid_spec=pltpu.PrefetchScalarGridSpec(
            num_scalar_prefetch=3,
            grid=(tiles,),
            in_specs=[
                pl.BlockSpec((slots, width, length), lambda i, *_: (0, 0, 0)),
                pl.BlockSpec((width, TILE), lambda i, *_: (0, chunk * tiles + i)),
            ]
            + [rows] * len(incoming),
            out_specs=rows,
        ),
        out_shape=jax.ShapeDtypeStruct((piece, width), dtype),
        compiler_params=pltpu.CompilerParams(vmem_limit_bytes=VMEM),
        cost_estimate=pl.CostEstimate(flops=cost, bytes_accessed=7_000_000, transcendentals=0),
        name="rest",
    )(offsets, counts, odd, estimate, observed, *incoming)


def filter_kernel(scale, x, inward, ahead, behind, first, second, outward, y):
    lines, steps, width = x.shape
    half = inward.shape[1] // 2
    rows = lines * GROUP
    spec = jnp.dot(
        x[...].reshape(lines * steps, width), inward[...], preferred_element_type=jnp.float32
    ).reshape(lines, steps, 2 * half)
    w1, w2 = first[...], second[...]
    backs = []
    for at in range(0, steps, GROUP):
        part = spec[:, at : at + GROUP, :].reshape(rows, 2 * half).astype(jnp.bfloat16)
        both = jnp.dot(ahead[...], part, preferred_element_type=jnp.float32)
        weighted_re = w1 * both[:rows, :half] + w2 * both[rows:, half:]
        weighted_im = w2 * both[:rows, half:] - w1 * both[rows:, :half]
        weighted = jnp.concatenate([weighted_re, weighted_im], axis=0).astype(jnp.bfloat16)
        back = jnp.dot(behind[...], weighted, preferred_element_type=jnp.float32)
        backs.append(jnp.concatenate([back[:rows], back[rows:]], axis=1).astype(jnp.bfloat16))
    total = jnp.dot(
        jnp.concatenate(backs, axis=0), outward[...], preferred_element_type=jnp.float32
    )
    total = (total * scale).reshape(steps // GROUP, lines, GROUP, width)
    y[...] = jnp.concatenate(list(total), axis=1).astype(jnp.bfloat16)


def filter_tables(coherence):
    lines, width = coherence.shape
    half = width // 2
    padded = -(-half // LANES) * LANES
    cos_inline, sin_inline = tables(width)
    cos_cross, sin_cross = tables(lines)
    opposite = jnp.roll(coherence[::-1, ::-1], (1, 1), (0, 1))
    weight = 0.5 * (coherence + opposite)
    lowest = np.arange(half)[None, :] == 0
    first = weight[:, :half]
    second = jnp.where(lowest, weight[:, half : half + 1], first)

    def pad(value):
        return np.pad(value, ((0, 0), (0, padded - half)))

    def spread(value):
        return jnp.repeat(jnp.pad(value, ((0, 0), (0, padded - half))), GROUP, axis=0)

    def constant(value):
        return jnp.asarray(value.astype(ml_dtypes.bfloat16))

    cos_half = cos_inline[:, :half]
    im_half = np.where(lowest, cos_inline[:, half : half + 1], -sin_inline[:, :half])
    inward = np.concatenate([pad(cos_half), pad(im_half)], axis=1)
    double = np.where(lowest, 1.0, 2.0)
    outward = np.concatenate([pad(cos_half * double), pad(im_half * double)], axis=1).T
    unit = np.eye(GROUP)
    cos_wide = np.kron(cos_cross, unit)
    sin_wide = np.kron(sin_cross, unit)
    behind = np.block([[cos_wide, -sin_wide], [sin_wide, cos_wide]])
    return (
        constant(inward),
        constant(np.concatenate([cos_wide, sin_wide], axis=0)),
        constant(behind),
        spread(first),
        spread(second),
        constant(outward),
    )


def filtered(x, prepared, chunk, chunks):
    lines, width = x.shape[0], x.shape[2]
    steps = x.shape[1] // chunks
    scale = 1.0 / (lines * width)
    tall = min(TALL, steps)
    held = [
        pl.BlockSpec(value.shape, lambda i, r=value.ndim: (0,) * r) for value in prepared
    ]
    out = pl.pallas_call(
        functools.partial(filter_kernel, scale),
        grid=(steps // tall,),
        in_specs=[
            pl.BlockSpec((lines, tall, width), lambda i: (0, chunk * (steps // tall) + i, 0))
        ]
        + held,
        out_specs=pl.BlockSpec((lines, tall, width), lambda i: (0, i, 0)),
        out_shape=jax.ShapeDtypeStruct((lines, steps, width), jnp.bfloat16),
        compiler_params=pltpu.CompilerParams(vmem_limit_bytes=VMEM),
        cost_estimate=pl.CostEstimate(
            flops=steps * 120_000_000, bytes_accessed=4 * x.size, transcendentals=0
        ),
        name="filter",
    )(x, *prepared)
    return out.reshape(lines * steps, width)


def update_kernel(places, first, offsets, counts, base, *refs):
    sources = refs[: len(places)]
    out, turned = refs[len(places) :]
    slots, width, tile = base.shape
    piece = sources[0].shape[0]
    span = turned.shape[1]
    window = tile + LANES
    step = first + pl.program_id(0)

    @pl.when(pl.program_id(0) == 0)
    def _():
        for at in range(first * tile // piece * piece, span, piece):
            size = min(piece, span - at)
            if at in places:
                source = sources[places.index(at)]
                for row in range(0, piece, TILE):
                    turned[:, pl.ds(at + row, TILE)] = source[pl.ds(row, TILE), :].T
            else:
                turned[:, pl.ds(at, size)] = jnp.zeros((width, size), jnp.bfloat16)

    row = lax.broadcasted_iota(jnp.int32, (window, tile), 0)
    column = lax.broadcasted_iota(jnp.int32, (window, tile), 1)
    for slot in range(slots):
        source_at = offsets[slot] + step * tile
        begin = source_at // LANES
        part = source_at - begin * LANES
        chosen = (row == column + part).astype(jnp.float32).astype(jnp.bfloat16)
        taken = turned[:, pl.ds(pl.multiple_of(begin * LANES, LANES), window)]
        moved = jnp.dot(taken, chosen, preferred_element_type=jnp.float32)
        total = base[slot].astype(jnp.float32) + moved
        out[slot] = jnp.where(slot < counts[0], total, 0.0).astype(jnp.bfloat16)


def update(base, sources, offsets, counts, first, in_place):
    slots, width, length = base.shape
    places = tuple(sorted(sources))
    arrays = [sources[place] for place in places]
    piece = arrays[0].shape[0]
    tiles = length // TILE - first
    spec = pl.BlockSpec((slots, width, TILE), lambda i, *_: (0, 0, first + i))
    whole = pl.BlockSpec((piece, width), lambda i, *_: (0, 0))
    return pl.pallas_call(
        functools.partial(update_kernel, places, first),
        grid_spec=pltpu.PrefetchScalarGridSpec(
            num_scalar_prefetch=2,
            grid=(tiles,),
            in_specs=[spec] + [whole] * len(arrays),
            out_specs=spec,
            scratch_shapes=[pltpu.VMEM((width, 2 * length), jnp.bfloat16)],
        ),
        out_shape=jax.ShapeDtypeStruct((slots, width, length), jnp.bfloat16),
        input_output_aliases={2: 0} if in_place else {},
        compiler_params=pltpu.CompilerParams(vmem_limit_bytes=VMEM),
        cost_estimate=pl.CostEstimate(
            flops=2_000_000_000, bytes_accessed=9_000_000, transcendentals=0
        ),
        name="update",
    )(offsets, counts, base, *arrays)


def body(estimate, observed, offsets, counts, coherence):
    slots, _, width, length = estimate.shape
    lines = lax.axis_size("line")
    blocks = lax.axis_size("block")
    odd = lax.axis_index("block") % 2 == 1
    odd_word = odd.astype(jnp.int32).reshape(1)
    swaps = [(i, i ^ 1) for i in range(blocks)]
    hops = [(i, i + 2) for i in range(0, blocks - 2, 2)]
    back_by_one = [(i + 1, i) for i in range(blocks - 1)]
    estimate = estimate.reshape(slots, width, length)
    observed = observed.reshape(width, length)
    prepared = filter_tables(coherence)
    tails = tails_of(estimate, offsets, counts)
    swapped = [lax.ppermute(tail, "block", swaps) for tail in tails]
    crossed = [lax.ppermute(tail, "block", hops) for tail in swapped]
    shot_args = (estimate, observed, offsets, counts, odd_word)
    spread = []
    for chunk in range(CHUNKS):
        if chunk == 0:
            rest = rest_of(*shot_args, chunk, [], jnp.float32, 3_000_000_000)
            incoming = jnp.where(odd, swapped[chunk], crossed[chunk]).astype(jnp.float32)
            residual = (rest - incoming).astype(jnp.bfloat16)
        else:
            residual = rest_of(
                *shot_args, chunk, [swapped[chunk], crossed[chunk]], jnp.bfloat16, 60_000_000_000
            )
        residual = residual.reshape(lines, -1, width)
        spread.append(lax.all_to_all(residual, "line", split_axis=0, concat_axis=0, tiled=True))
    piece = length // CHUNKS
    sources = {}
    updated = estimate
    for chunk in range(CHUNKS):
        back = filtered(spread[chunk], prepared, 0, 1)
        back = lax.all_to_all(back, "line", split_axis=0, concat_axis=0, tiled=True)
        following = lax.ppermute(back, "block", back_by_one)
        sources[chunk * piece] = back
        if chunk == CHUNKS - 1:
            updated = update(updated, sources, offsets, counts, 0, False)
            sources = {}
        sources[length + chunk * piece] = following
    last = (length - piece) // TILE
    updated = update(updated, sources, offsets, counts, last, True)
    return updated.reshape(slots, 1, width, length)


def solution(mesh):
    return jax.shard_map(
        body,
        mesh=mesh,
        in_specs=(
            P("block", "line", None, None),
            P("line", None, "block"),
            P("block"),
            P("block"),
            P(),
        ),
        out_specs=P("block", "line", None, None),
        check_vma=False,
    )
```

```python
import functools
import math

import jax
import jax.numpy as jnp
import ml_dtypes
import numpy as np
from jax import lax
from jax.experimental import pallas as pl
from jax.experimental.pallas import tpu as pltpu
from jax.sharding import PartitionSpec as P

CHUNKS = 2
TILE = 256
LANES = 128
GROUP = 8
TALL = 32
VMEM = 48 * 1024 * 1024
TALL_VMEM = 60 * 1024 * 1024


def tables(count):
    position = np.arange(count, dtype=np.int32)
    product = position[:, None] * position[None, :] % count
    angle = product.astype(np.float32) * np.float32(2.0 * math.pi / count)
    rounded = lambda value: value.astype(ml_dtypes.bfloat16).astype(np.float32)
    return (rounded(np.cos(angle)), rounded(np.sin(angle)))


def rows_by_rows(left, right):
    return lax.dot_general(
        left, right, (((1,), (1,)), ((), ())), preferred_element_type=jnp.float32
    )


def part_of(offset, length):
    return lax.rem(length - offset, LANES)


def choose_shots(offsets, counts, length, chosen):
    @pl.when(pl.program_id(0) == 0)
    def _():
        slots, tile, window = chosen.shape
        row = lax.broadcasted_iota(jnp.int32, (tile, window), 0)
        column = lax.broadcasted_iota(jnp.int32, (tile, window), 1)
        for slot in range(slots):
            value = jnp.where(slot < counts[0], 1.0, 0.0).astype(jnp.float32)
            part = part_of(offsets[slot], length)
            chosen[slot] = jnp.where(column == row + part, value, 0.0).astype(jnp.bfloat16)


def turned_shots(first, tile, offsets, estimate, chosen):
    slots, width, length = estimate.shape
    blocks = length // LANES
    window = tile // LANES + 1
    time = first + lax.broadcasted_iota(jnp.int32, (tile, width), 0)
    for slot in range(slots):
        offset = offsets[slot]
        begin = lax.rem(first - offset + length, length) // LANES
        pieces = [
            estimate[slot, :, pl.ds(pl.multiple_of(lax.rem(begin + j, blocks) * LANES, LANES), LANES)]
            for j in range(window)
        ]
        yield time >= offset, rows_by_rows(chosen[slot], jnp.concatenate(pieces, axis=1))


def shifted(pieces, by):
    lane = lax.broadcasted_iota(jnp.int32, pieces[0].shape, 1)
    turned = [pltpu.roll(piece, by, 1) for piece in pieces]
    return jnp.concatenate(
        [jnp.where(lane < by, low, high) for low, high in zip(turned, turned[1:])], axis=1
    )


def shifted_back(pieces, by):
    lane = lax.broadcasted_iota(jnp.int32, pieces[0].shape, 1)
    turned = [pltpu.roll(piece, lax.rem(LANES - by, LANES), 1) for piece in pieces]
    return jnp.concatenate(
        [jnp.where(lane < LANES - by, low, high) for low, high in zip(turned, turned[1:])], axis=1
    )


def rolled_shots(offsets, counts, estimate, span):
    slots, rows, length = estimate.shape
    blocks = length // LANES
    time = lax.broadcasted_iota(jnp.int32, (rows, span), 1)
    for slot in range(slots):
        offset = offsets[slot]
        behind_by = blocks - 1 - offset // LANES
        pieces = [
            estimate[slot, :, pl.ds(pl.multiple_of(lax.rem(behind_by + j, blocks) * LANES, LANES), LANES)]
            for j in range(span // LANES + 1)
        ]
        moved = shifted(pieces, lax.rem(offset, LANES)).astype(jnp.float32)
        live = slot < counts[0]
        ahead = jnp.where(live & (time >= offset), moved, 0.0)
        behind = jnp.where(live & (time < offset), moved, 0.0)
        yield ahead, behind


def tail_kernel(offsets, counts, estimate, *tails):
    total = sum(
        behind for _, behind in rolled_shots(offsets, counts, estimate, estimate.shape[2])
    )
    total = total.astype(jnp.bfloat16)
    piece = tails[0].shape[0]
    for chunk, tail in enumerate(tails):
        tail[...] = total[:, chunk * piece : (chunk + 1) * piece].T


def tails_of(estimate, offsets, counts):
    slots, width, length = estimate.shape
    piece = length // CHUNKS
    return pl.pallas_call(
        tail_kernel,
        grid_spec=pltpu.PrefetchScalarGridSpec(
            num_scalar_prefetch=2,
            grid=(width // LANES,),
            in_specs=[pl.BlockSpec((slots, LANES, length), lambda i, *_: (0, i, 0))],
            out_specs=[pl.BlockSpec((piece, LANES), lambda i, *_: (0, i))] * CHUNKS,
        ),
        out_shape=[jax.ShapeDtypeStruct((piece, width), jnp.bfloat16)] * CHUNKS,
        compiler_params=pltpu.CompilerParams(vmem_limit_bytes=TALL_VMEM),
        cost_estimate=pl.CostEstimate(
            flops=3_000_000_000, bytes_accessed=5_000_000, transcendentals=0
        ),
        name="tails",
    )(offsets, counts, estimate)


def lead_kernel(offsets, counts, estimate, observed, rest):
    piece = rest.shape[0]
    total = sum(ahead for ahead, _ in rolled_shots(offsets, counts, estimate, piece))
    rest[...] = (observed[...].astype(jnp.float32) - total).T


def lead_of(estimate, observed, offsets, counts):
    slots, width, length = estimate.shape
    piece = length // CHUNKS
    return pl.pallas_call(
        lead_kernel,
        grid_spec=pltpu.PrefetchScalarGridSpec(
            num_scalar_prefetch=2,
            grid=(width // LANES,),
            in_specs=[
                pl.BlockSpec((slots, LANES, length), lambda i, *_: (0, i, 0)),
                pl.BlockSpec((LANES, piece), lambda i, *_: (i, 0)),
            ],
            out_specs=pl.BlockSpec((piece, LANES), lambda i, *_: (0, i)),
        ),
        out_shape=jax.ShapeDtypeStruct((piece, width), jnp.float32),
        compiler_params=pltpu.CompilerParams(vmem_limit_bytes=VMEM),
        cost_estimate=pl.CostEstimate(
            flops=3_000_000_000, bytes_accessed=7_000_000, transcendentals=0
        ),
        name="lead",
    )(offsets, counts, estimate, observed)


def rest_kernel(begin_at, offsets, counts, odd, estimate, observed, *refs):
    *incoming, out, chosen, unit = refs
    tile, width = out.shape
    first = begin_at + pl.program_id(0) * tile
    choose_shots(offsets, counts, estimate.shape[2], chosen)

    @pl.when(pl.program_id(0) == 0)
    def _():
        row = lax.broadcasted_iota(jnp.int32, (tile, tile), 0)
        column = lax.broadcasted_iota(jnp.int32, (tile, tile), 1)
        unit[...] = (row == column).astype(jnp.float32).astype(jnp.bfloat16)

    ahead = rows_by_rows(unit[...], observed[...])
    for here, moved in turned_shots(first, tile, offsets, estimate, chosen):
        ahead = ahead - jnp.where(here, moved, 0.0)
    if incoming:
        swapped, crossed = (ref[...].astype(jnp.float32) for ref in incoming)
        ahead = ahead - jnp.where(odd[0] == 1, swapped, crossed)
    out[...] = ahead.astype(out.dtype)


def rest_of(estimate, observed, offsets, counts, odd, chunk, incoming, dtype, cost):
    slots, width, length = estimate.shape
    piece = length // CHUNKS
    tiles = piece // TILE
    rows = pl.BlockSpec((TILE, width), lambda i, *_: (i, 0))
    return pl.pallas_call(
        functools.partial(rest_kernel, chunk * piece),
        grid_spec=pltpu.PrefetchScalarGridSpec(
            num_scalar_prefetch=3,
            grid=(tiles,),
            in_specs=[
                pl.BlockSpec((slots, width, length), lambda i, *_: (0, 0, 0)),
                pl.BlockSpec((width, TILE), lambda i, *_: (0, chunk * tiles + i)),
            ]
            + [rows] * len(incoming),
            out_specs=rows,
            scratch_shapes=[
                pltpu.VMEM((slots, TILE, TILE + LANES), jnp.bfloat16),
                pltpu.VMEM((TILE, TILE), jnp.bfloat16),
            ],
        ),
        out_shape=jax.ShapeDtypeStruct((piece, width), dtype),
        compiler_params=pltpu.CompilerParams(vmem_limit_bytes=VMEM),
        cost_estimate=pl.CostEstimate(flops=cost, bytes_accessed=7_000_000, transcendentals=0),
        name="rest",
    )(offsets, counts, odd, estimate, observed, *incoming)


def filter_kernel(scale, x, inward, ahead, behind, first, second, outward, y):
    lines, steps, width = x.shape
    half = inward.shape[1] // 2
    rows = lines * GROUP
    spec = jnp.dot(
        x[...].reshape(lines * steps, width), inward[...], preferred_element_type=jnp.float32
    ).reshape(lines, steps, 2 * half)
    w1, w2 = first[...], second[...]
    backs = []
    for at in range(0, steps, GROUP):
        part = spec[:, at : at + GROUP, :].reshape(rows, 2 * half).astype(jnp.bfloat16)
        both = jnp.dot(ahead[...], part, preferred_element_type=jnp.float32)
        weighted_re = w1 * both[:rows, :half] + w2 * both[rows:, half:]
        weighted_im = w2 * both[:rows, half:] - w1 * both[rows:, :half]
        weighted = jnp.concatenate([weighted_re, weighted_im], axis=0).astype(jnp.bfloat16)
        back = jnp.dot(behind[...], weighted, preferred_element_type=jnp.float32)
        backs.append(jnp.concatenate([back[:rows], back[rows:]], axis=1).astype(jnp.bfloat16))
    total = jnp.dot(
        jnp.concatenate(backs, axis=0), outward[...], preferred_element_type=jnp.float32
    )
    total = (total * scale).reshape(steps // GROUP, lines, GROUP, width)
    y[...] = jnp.concatenate(list(total), axis=1).astype(jnp.bfloat16)


def filter_tables(coherence):
    lines, width = coherence.shape
    half = width // 2
    padded = -(-half // LANES) * LANES
    cos_inline, sin_inline = tables(width)
    cos_cross, sin_cross = tables(lines)
    opposite = jnp.roll(coherence[::-1, ::-1], (1, 1), (0, 1))
    weight = 0.5 * (coherence + opposite)
    lowest = np.arange(half)[None, :] == 0
    first = weight[:, :half]
    second = jnp.where(lowest, weight[:, half : half + 1], first)

    def pad(value):
        return np.pad(value, ((0, 0), (0, padded - half)))

    def spread(value):
        return jnp.repeat(jnp.pad(value, ((0, 0), (0, padded - half))), GROUP, axis=0)

    def constant(value):
        return jnp.asarray(value.astype(ml_dtypes.bfloat16))

    cos_half = cos_inline[:, :half]
    im_half = np.where(lowest, cos_inline[:, half : half + 1], -sin_inline[:, :half])
    inward = np.concatenate([pad(cos_half), pad(im_half)], axis=1)
    double = np.where(lowest, 1.0, 2.0)
    outward = np.concatenate([pad(cos_half * double), pad(im_half * double)], axis=1).T
    unit = np.eye(GROUP)
    cos_wide = np.kron(cos_cross, unit)
    sin_wide = np.kron(sin_cross, unit)
    behind = np.block([[cos_wide, -sin_wide], [sin_wide, cos_wide]])
    return (
        constant(inward),
        constant(np.concatenate([cos_wide, sin_wide], axis=0)),
        constant(behind),
        spread(first),
        spread(second),
        constant(outward),
    )


def filtered(x, prepared, chunk, chunks):
    lines, width = x.shape[0], x.shape[2]
    steps = x.shape[1] // chunks
    scale = 1.0 / (lines * width)
    tall = min(TALL, steps)
    held = [
        pl.BlockSpec(value.shape, lambda i, r=value.ndim: (0,) * r) for value in prepared
    ]
    out = pl.pallas_call(
        functools.partial(filter_kernel, scale),
        grid=(steps // tall,),
        in_specs=[
            pl.BlockSpec((lines, tall, width), lambda i: (0, chunk * (steps // tall) + i, 0))
        ]
        + held,
        out_specs=pl.BlockSpec((lines, tall, width), lambda i: (0, i, 0)),
        out_shape=jax.ShapeDtypeStruct((lines, steps, width), jnp.bfloat16),
        compiler_params=pltpu.CompilerParams(vmem_limit_bytes=VMEM),
        cost_estimate=pl.CostEstimate(
            flops=steps * 120_000_000, bytes_accessed=4 * x.size, transcendentals=0
        ),
        name="filter",
    )(x, *prepared)
    return out.reshape(lines * steps, width)


def update_kernel(places, first, offsets, counts, base, *refs):
    *sources, out, turned, chosen = refs
    slots, width, tile = base.shape
    piece = sources[0].shape[0]
    span = turned.shape[1]
    window = tile + LANES
    low, high = places[0], places[-1] + piece
    step = first + pl.program_id(0)

    @pl.when(pl.program_id(0) == 0)
    def _():
        if low > 0:
            turned[:, pl.ds(low - window, window)] = jnp.zeros((width, window), jnp.bfloat16)
        if high < span:
            turned[:, pl.ds(high, window)] = jnp.zeros((width, window), jnp.bfloat16)
        for source, at in zip(sources, places):
            for row in range(0, piece, TILE):
                turned[:, pl.ds(at + row, TILE)] = source[pl.ds(row, TILE), :].T
        row = lax.broadcasted_iota(jnp.int32, (window, tile), 0)
        column = lax.broadcasted_iota(jnp.int32, (window, tile), 1)
        for slot in range(slots):
            part = lax.rem(offsets[slot], LANES)
            chosen[slot] = (row == column + part).astype(jnp.float32).astype(jnp.bfloat16)

    for slot in range(slots):
        source_at = offsets[slot] + step * tile
        live = slot < counts[0]
        touched = live & (source_at + tile > low) & (source_at < high)

        @pl.when(touched)
        def _(slot=slot, source_at=source_at):
            begin = source_at // LANES
            taken = turned[:, pl.ds(pl.multiple_of(begin * LANES, LANES), window)]
            moved = jnp.dot(taken, chosen[slot], preferred_element_type=jnp.float32)
            out[slot] = (base[slot].astype(jnp.float32) + moved).astype(jnp.bfloat16)

        @pl.when(jnp.logical_not(touched))
        def _(slot=slot):
            out[slot] = jnp.where(live, base[slot], jnp.zeros_like(base[slot]))


def update(base, sources, offsets, counts, first, in_place):
    slots, width, length = base.shape
    places = tuple(sorted(sources))
    arrays = [sources[place] for place in places]
    piece = arrays[0].shape[0]
    tiles = length // TILE - first
    spec = pl.BlockSpec((slots, width, TILE), lambda i, *_: (0, 0, first + i))
    whole = pl.BlockSpec((piece, width), lambda i, *_: (0, 0))
    return pl.pallas_call(
        functools.partial(update_kernel, places, first),
        grid_spec=pltpu.PrefetchScalarGridSpec(
            num_scalar_prefetch=2,
            grid=(tiles,),
            in_specs=[spec] + [whole] * len(arrays),
            out_specs=spec,
            scratch_shapes=[
                pltpu.VMEM((width, 2 * length), jnp.bfloat16),
                pltpu.VMEM((slots, TILE + LANES, TILE), jnp.bfloat16),
            ],
        ),
        out_shape=jax.ShapeDtypeStruct((slots, width, length), jnp.bfloat16),
        input_output_aliases={2: 0} if in_place else {},
        compiler_params=pltpu.CompilerParams(vmem_limit_bytes=VMEM),
        cost_estimate=pl.CostEstimate(
            flops=2_000_000_000, bytes_accessed=9_000_000, transcendentals=0
        ),
        name="update",
    )(offsets, counts, base, *arrays)


def finish_kernel(offsets, counts, base, last, out, turned):
    slots, rows, piece = base.shape
    span = turned.shape[1]
    blank = span - piece
    turned[:, :blank] = jnp.zeros((rows, blank), jnp.bfloat16)
    turned[:, blank:] = last[...].T
    for slot in range(slots):
        begin = jnp.maximum(offsets[slot] - piece, 0) // LANES
        pieces = [
            turned[:, pl.ds(pl.multiple_of((begin + j) * LANES, LANES), LANES)]
            for j in range(piece // LANES + 1)
        ]
        moved = shifted_back(pieces, lax.rem(offsets[slot], LANES)).astype(jnp.float32)
        live = slot < counts[0]
        mine = live & (offsets[slot] > piece)
        total = base[slot].astype(jnp.float32) + jnp.where(mine, moved, 0.0)
        out[slot] = jnp.where(live, total, 0.0).astype(jnp.bfloat16)


def finish(base, last, offsets, counts):
    slots, width, length = base.shape
    piece = last.shape[0]
    spec = pl.BlockSpec((slots, LANES, piece), lambda i, *_: (0, i, length // piece - 1))
    return pl.pallas_call(
        finish_kernel,
        grid_spec=pltpu.PrefetchScalarGridSpec(
            num_scalar_prefetch=2,
            grid=(width // LANES,),
            in_specs=[spec, pl.BlockSpec((piece, LANES), lambda i, *_: (0, i))],
            out_specs=spec,
            scratch_shapes=[pltpu.VMEM((LANES, 2 * piece), jnp.bfloat16)],
        ),
        out_shape=jax.ShapeDtypeStruct((slots, width, length), jnp.bfloat16),
        input_output_aliases={2: 0},
        compiler_params=pltpu.CompilerParams(vmem_limit_bytes=VMEM),
        cost_estimate=pl.CostEstimate(
            flops=10_000_000, bytes_accessed=4_000_000, transcendentals=0
        ),
        name="finish",
    )(offsets, counts, base, last)


def body(estimate, observed, offsets, counts, coherence):
    slots, _, width, length = estimate.shape
    lines = lax.axis_size("line")
    blocks = lax.axis_size("block")
    odd = lax.axis_index("block") % 2 == 1
    odd_word = odd.astype(jnp.int32).reshape(1)
    swaps = [(i, i ^ 1) for i in range(blocks)]
    hops = [(i, i + 2) for i in range(0, blocks - 2, 2)]
    back_by_one = [(i + 1, i) for i in range(blocks - 1)]
    estimate = estimate.reshape(slots, width, length)
    observed = observed.reshape(width, length)
    prepared = filter_tables(coherence)
    tails = tails_of(estimate, offsets, counts)
    swapped = [lax.ppermute(tail, "block", swaps) for tail in tails]
    crossed = [lax.ppermute(tail, "block", hops) for tail in swapped]
    shot_args = (estimate, observed, offsets, counts, odd_word)
    spread = []
    for chunk in range(CHUNKS):
        if chunk == 0:
            rest = lead_of(estimate, observed, offsets, counts)
            incoming = jnp.where(odd, swapped[chunk], crossed[chunk]).astype(jnp.float32)
            residual = (rest - incoming).astype(jnp.bfloat16)
        else:
            residual = rest_of(
                *shot_args, chunk, [swapped[chunk], crossed[chunk]], jnp.bfloat16, 60_000_000_000
            )
        residual = residual.reshape(lines, -1, width)
        spread.append(lax.all_to_all(residual, "line", split_axis=0, concat_axis=0, tiled=True))
    piece = length // CHUNKS
    sources = {}
    updated = estimate
    for chunk in range(CHUNKS):
        back = filtered(spread[chunk], prepared, 0, 1)
        back = lax.all_to_all(back, "line", split_axis=0, concat_axis=0, tiled=True)
        following = lax.ppermute(back, "block", back_by_one)
        sources[chunk * piece] = back
        if chunk == CHUNKS - 1:
            updated = update(updated, sources, offsets, counts, 0, False)
            sources = {}
        sources[length + chunk * piece] = following
    updated = finish(updated, following, offsets, counts)
    return updated.reshape(slots, 1, width, length)


def solution(mesh):
    return jax.shard_map(
        body,
        mesh=mesh,
        in_specs=(
            P("block", "line", None, None),
            P("line", None, "block"),
            P("block"),
            P("block"),
            P(),
        ),
        out_specs=P("block", "line", None, None),
        check_vma=False,
    )
```

```python
import functools
import math

import jax
import jax.numpy as jnp
import ml_dtypes
import numpy as np
from jax import lax
from jax.experimental import pallas as pl
from jax.experimental.pallas import tpu as pltpu
from jax.sharding import PartitionSpec as P

CHUNKS = 2
WIDE = 512
LANES = 128
GROUP = 8
TALL = 32
VMEM = 48 * 1024 * 1024
TALL_VMEM = 60 * 1024 * 1024


def tables(count):
    position = np.arange(count, dtype=np.int32)
    product = position[:, None] * position[None, :] % count
    angle = product.astype(np.float32) * np.float32(2.0 * math.pi / count)
    rounded = lambda value: value.astype(ml_dtypes.bfloat16).astype(np.float32)
    return (rounded(np.cos(angle)), rounded(np.sin(angle)))


def shifted(pieces, by):
    lane = lax.broadcasted_iota(jnp.int32, pieces[0].shape, 1)
    turned = [pltpu.roll(piece, by, 1) for piece in pieces]
    return jnp.concatenate(
        [jnp.where(lane < by, low, high) for low, high in zip(turned, turned[1:])], axis=1
    )


def shifted_back(pieces, by):
    lane = lax.broadcasted_iota(jnp.int32, pieces[0].shape, 1)
    turned = [pltpu.roll(piece, lax.rem(LANES - by, LANES), 1) for piece in pieces]
    return jnp.concatenate(
        [jnp.where(lane < LANES - by, low, high) for low, high in zip(turned, turned[1:])], axis=1
    )


def rolled_shots(offsets, counts, estimate, span):
    slots, rows, length = estimate.shape
    blocks = length // LANES
    time = lax.broadcasted_iota(jnp.int32, (rows, span), 1)
    for slot in range(slots):
        offset = offsets[slot]
        behind_by = blocks - 1 - offset // LANES
        pieces = [
            estimate[slot, :, pl.ds(pl.multiple_of(lax.rem(behind_by + j, blocks) * LANES, LANES), LANES)]
            for j in range(span // LANES + 1)
        ]
        moved = shifted(pieces, lax.rem(offset, LANES)).astype(jnp.float32)
        live = slot < counts[0]
        ahead = jnp.where(live & (time >= offset), moved, 0.0)
        behind = jnp.where(live & (time < offset), moved, 0.0)
        yield ahead, behind


def tail_kernel(offsets, counts, estimate, *tails):
    total = sum(
        behind for _, behind in rolled_shots(offsets, counts, estimate, estimate.shape[2])
    )
    total = total.astype(jnp.bfloat16)
    piece = tails[0].shape[0]
    for chunk, tail in enumerate(tails):
        tail[...] = total[:, chunk * piece : (chunk + 1) * piece].T


def tails_of(estimate, offsets, counts):
    slots, width, length = estimate.shape
    piece = length // CHUNKS
    return pl.pallas_call(
        tail_kernel,
        grid_spec=pltpu.PrefetchScalarGridSpec(
            num_scalar_prefetch=2,
            grid=(width // LANES,),
            in_specs=[pl.BlockSpec((slots, LANES, length), lambda i, *_: (0, i, 0))],
            out_specs=[pl.BlockSpec((piece, LANES), lambda i, *_: (0, i))] * CHUNKS,
        ),
        out_shape=[jax.ShapeDtypeStruct((piece, width), jnp.bfloat16)] * CHUNKS,
        compiler_params=pltpu.CompilerParams(vmem_limit_bytes=TALL_VMEM),
        cost_estimate=pl.CostEstimate(
            flops=3_000_000_000, bytes_accessed=5_000_000, transcendentals=0
        ),
        name="tails",
    )(offsets, counts, estimate)


def lead_kernel(offsets, counts, estimate, observed, rest):
    piece = rest.shape[0]
    total = sum(ahead for ahead, _ in rolled_shots(offsets, counts, estimate, piece))
    rest[...] = (observed[...].astype(jnp.float32) - total).T


def lead_of(estimate, observed, offsets, counts):
    slots, width, length = estimate.shape
    piece = length
    return pl.pallas_call(
        lead_kernel,
        grid_spec=pltpu.PrefetchScalarGridSpec(
            num_scalar_prefetch=2,
            grid=(width // LANES,),
            in_specs=[
                pl.BlockSpec((slots, LANES, length), lambda i, *_: (0, i, 0)),
                pl.BlockSpec((LANES, piece), lambda i, *_: (i, 0)),
            ],
            out_specs=pl.BlockSpec((piece, LANES), lambda i, *_: (0, i)),
        ),
        out_shape=jax.ShapeDtypeStruct((piece, width), jnp.float32),
        compiler_params=pltpu.CompilerParams(vmem_limit_bytes=VMEM),
        cost_estimate=pl.CostEstimate(
            flops=3_000_000_000, bytes_accessed=7_000_000, transcendentals=0
        ),
        name="lead",
    )(offsets, counts, estimate, observed)


def filter_kernel(scale, x, inward, ahead, behind, first, second, outward, y):
    lines, steps, width = x.shape
    half = inward.shape[1] // 2
    rows = lines * GROUP
    spec = jnp.dot(
        x[...].reshape(lines * steps, width), inward[...], preferred_element_type=jnp.float32
    ).reshape(lines, steps, 2 * half)
    w1, w2 = first[...], second[...]
    backs = []
    for at in range(0, steps, GROUP):
        part = spec[:, at : at + GROUP, :].reshape(rows, 2 * half).astype(jnp.bfloat16)
        both = jnp.dot(ahead[...], part, preferred_element_type=jnp.float32)
        weighted_re = w1 * both[:rows, :half] + w2 * both[rows:, half:]
        weighted_im = w2 * both[:rows, half:] - w1 * both[rows:, :half]
        weighted = jnp.concatenate([weighted_re, weighted_im], axis=0).astype(jnp.bfloat16)
        back = jnp.dot(behind[...], weighted, preferred_element_type=jnp.float32)
        backs.append(jnp.concatenate([back[:rows], back[rows:]], axis=1).astype(jnp.bfloat16))
    total = jnp.dot(
        jnp.concatenate(backs, axis=0), outward[...], preferred_element_type=jnp.float32
    )
    total = (total * scale).reshape(steps // GROUP, lines, GROUP, width)
    y[...] = jnp.concatenate(list(total), axis=1).astype(jnp.bfloat16)


def filter_tables(coherence):
    lines, width = coherence.shape
    half = width // 2
    padded = -(-half // LANES) * LANES
    cos_inline, sin_inline = tables(width)
    cos_cross, sin_cross = tables(lines)
    opposite = jnp.roll(coherence[::-1, ::-1], (1, 1), (0, 1))
    weight = 0.5 * (coherence + opposite)
    lowest = np.arange(half)[None, :] == 0
    first = weight[:, :half]
    second = jnp.where(lowest, weight[:, half : half + 1], first)

    def pad(value):
        return np.pad(value, ((0, 0), (0, padded - half)))

    def spread(value):
        return jnp.repeat(jnp.pad(value, ((0, 0), (0, padded - half))), GROUP, axis=0)

    def constant(value):
        return jnp.asarray(value.astype(ml_dtypes.bfloat16))

    cos_half = cos_inline[:, :half]
    im_half = np.where(lowest, cos_inline[:, half : half + 1], -sin_inline[:, :half])
    inward = np.concatenate([pad(cos_half), pad(im_half)], axis=1)
    double = np.where(lowest, 1.0, 2.0)
    outward = np.concatenate([pad(cos_half * double), pad(im_half * double)], axis=1).T
    unit = np.eye(GROUP)
    cos_wide = np.kron(cos_cross, unit)
    sin_wide = np.kron(sin_cross, unit)
    behind = np.block([[cos_wide, -sin_wide], [sin_wide, cos_wide]])
    return (
        constant(inward),
        constant(np.concatenate([cos_wide, sin_wide], axis=0)),
        constant(behind),
        spread(first),
        spread(second),
        constant(outward),
    )


def filtered(x, prepared, chunk, chunks):
    lines, width = x.shape[0], x.shape[2]
    steps = x.shape[1] // chunks
    scale = 1.0 / (lines * width)
    tall = min(TALL, steps)
    held = [
        pl.BlockSpec(value.shape, lambda i, r=value.ndim: (0,) * r) for value in prepared
    ]
    out = pl.pallas_call(
        functools.partial(filter_kernel, scale),
        grid=(steps // tall,),
        in_specs=[
            pl.BlockSpec((lines, tall, width), lambda i: (0, chunk * (steps // tall) + i, 0))
        ]
        + held,
        out_specs=pl.BlockSpec((lines, tall, width), lambda i: (0, i, 0)),
        out_shape=jax.ShapeDtypeStruct((lines, steps, width), jnp.bfloat16),
        compiler_params=pltpu.CompilerParams(vmem_limit_bytes=VMEM),
        cost_estimate=pl.CostEstimate(
            flops=steps * 120_000_000, bytes_accessed=4 * x.size, transcendentals=0
        ),
        name="filter",
    )(x, *prepared)
    return out.reshape(lines * steps, width)


def update_kernel(places, first, offsets, counts, base, *refs):
    *sources, out, turned, chosen = refs
    slots, width, tile = base.shape
    piece = sources[0].shape[0]
    span = turned.shape[1]
    window = tile + LANES
    low, high = places[0], places[-1] + piece
    step = first + pl.program_id(0)

    @pl.when(pl.program_id(0) == 0)
    def _():
        if low > 0:
            turned[:, pl.ds(low - window, window)] = jnp.zeros((width, window), jnp.bfloat16)
        if high < span:
            turned[:, pl.ds(high, window)] = jnp.zeros((width, window), jnp.bfloat16)
        for source, at in zip(sources, places):
            for row in range(0, piece, tile):
                turned[:, pl.ds(at + row, tile)] = source[pl.ds(row, tile), :].T
        row = lax.broadcasted_iota(jnp.int32, (window, tile), 0)
        column = lax.broadcasted_iota(jnp.int32, (window, tile), 1)
        for slot in range(slots):
            part = lax.rem(offsets[slot], LANES)
            chosen[slot] = (row == column + part).astype(jnp.float32).astype(jnp.bfloat16)

    for slot in range(slots):
        source_at = offsets[slot] + step * tile
        live = slot < counts[0]
        touched = live & (source_at + tile > low) & (source_at < high)

        @pl.when(touched)
        def _(slot=slot, source_at=source_at):
            begin = source_at // LANES
            taken = turned[:, pl.ds(pl.multiple_of(begin * LANES, LANES), window)]
            moved = jnp.dot(taken, chosen[slot], preferred_element_type=jnp.float32)
            out[slot] = (base[slot].astype(jnp.float32) + moved).astype(jnp.bfloat16)

        @pl.when(jnp.logical_not(touched))
        def _(slot=slot):
            out[slot] = jnp.where(live, base[slot], jnp.zeros_like(base[slot]))


def update(base, sources, offsets, counts, first, in_place):
    slots, width, length = base.shape
    places = tuple(sorted(sources))
    arrays = [sources[place] for place in places]
    piece = arrays[0].shape[0]
    tiles = length // WIDE - first
    spec = pl.BlockSpec((slots, width, WIDE), lambda i, *_: (0, 0, first + i))
    whole = pl.BlockSpec((piece, width), lambda i, *_: (0, 0))
    return pl.pallas_call(
        functools.partial(update_kernel, places, first),
        grid_spec=pltpu.PrefetchScalarGridSpec(
            num_scalar_prefetch=2,
            grid=(tiles,),
            in_specs=[spec] + [whole] * len(arrays),
            out_specs=spec,
            scratch_shapes=[
                pltpu.VMEM((width, 2 * length), jnp.bfloat16),
                pltpu.VMEM((slots, WIDE + LANES, WIDE), jnp.bfloat16),
            ],
        ),
        out_shape=jax.ShapeDtypeStruct((slots, width, length), jnp.bfloat16),
        input_output_aliases={2: 0} if in_place else {},
        compiler_params=pltpu.CompilerParams(vmem_limit_bytes=VMEM),
        cost_estimate=pl.CostEstimate(
            flops=2_000_000_000, bytes_accessed=9_000_000, transcendentals=0
        ),
        name="update",
    )(offsets, counts, base, *arrays)


def finish_kernel(offsets, counts, base, last, out, turned):
    slots, rows, piece = base.shape
    span = turned.shape[1]
    blank = span - piece
    turned[:, :blank] = jnp.zeros((rows, blank), jnp.bfloat16)
    turned[:, blank:] = last[...].T
    for slot in range(slots):
        begin = jnp.maximum(offsets[slot] - piece, 0) // LANES
        pieces = [
            turned[:, pl.ds(pl.multiple_of((begin + j) * LANES, LANES), LANES)]
            for j in range(piece // LANES + 1)
        ]
        moved = shifted_back(pieces, lax.rem(offsets[slot], LANES)).astype(jnp.float32)
        live = slot < counts[0]
        mine = live & (offsets[slot] > piece)
        total = base[slot].astype(jnp.float32) + jnp.where(mine, moved, 0.0)
        out[slot] = jnp.where(live, total, 0.0).astype(jnp.bfloat16)


def finish(base, last, offsets, counts):
    slots, width, length = base.shape
    piece = last.shape[0]
    spec = pl.BlockSpec((slots, width, piece), lambda i, *_: (0, i, length // piece - 1))
    return pl.pallas_call(
        finish_kernel,
        grid_spec=pltpu.PrefetchScalarGridSpec(
            num_scalar_prefetch=2,
            grid=(width // width,),
            in_specs=[spec, pl.BlockSpec((piece, width), lambda i, *_: (0, i))],
            out_specs=spec,
            scratch_shapes=[pltpu.VMEM((width, 2 * piece), jnp.bfloat16)],
        ),
        out_shape=jax.ShapeDtypeStruct((slots, width, length), jnp.bfloat16),
        input_output_aliases={2: 0},
        compiler_params=pltpu.CompilerParams(vmem_limit_bytes=VMEM),
        cost_estimate=pl.CostEstimate(
            flops=10_000_000, bytes_accessed=4_000_000, transcendentals=0
        ),
        name="finish",
    )(offsets, counts, base, last)


def body(estimate, observed, offsets, counts, coherence):
    slots, _, width, length = estimate.shape
    lines = lax.axis_size("line")
    blocks = lax.axis_size("block")
    odd = lax.axis_index("block") % 2 == 1
    swaps = [(i, i ^ 1) for i in range(blocks)]
    hops = [(i, i + 2) for i in range(0, blocks - 2, 2)]
    back_by_one = [(i + 1, i) for i in range(blocks - 1)]
    estimate = estimate.reshape(slots, width, length)
    observed = observed.reshape(width, length)
    prepared = filter_tables(coherence)
    tails = tails_of(estimate, offsets, counts)
    swapped = [lax.ppermute(tail, "block", swaps) for tail in tails]
    crossed = [lax.ppermute(tail, "block", hops) for tail in swapped]
    rest = lead_of(estimate, observed, offsets, counts)
    incoming = jnp.concatenate(
        [jnp.where(odd, beside, before) for beside, before in zip(swapped, crossed)], axis=0
    )
    residual = (rest - incoming.astype(jnp.float32)).astype(jnp.bfloat16)
    residual = residual.reshape(lines, -1, width)
    spread = lax.all_to_all(residual, "line", split_axis=0, concat_axis=0, tiled=True)
    own = filtered(spread, prepared, 0, 1)
    own = lax.all_to_all(own, "line", split_axis=0, concat_axis=0, tiled=True)
    piece = length // CHUNKS
    own = [own[chunk * piece : (chunk + 1) * piece] for chunk in range(CHUNKS)]
    following = [lax.ppermute(part, "block", back_by_one) for part in own]
    sources = {at * piece: part for at, part in enumerate(own + following[:-1])}
    updated = update(estimate, sources, offsets, counts, 0, False)
    updated = finish(updated, following[-1], offsets, counts)
    return updated.reshape(slots, 1, width, length)


def solution(mesh):
    return jax.shard_map(
        body,
        mesh=mesh,
        in_specs=(
            P("block", "line", None, None),
            P("line", None, "block"),
            P("block"),
            P("block"),
            P(),
        ),
        out_specs=P("block", "line", None, None),
        check_vma=False,
    )
```

```python
import functools
import math

import jax
import jax.numpy as jnp
import ml_dtypes
import numpy as np
from jax import lax
from jax.experimental import pallas as pl
from jax.experimental.pallas import tpu as pltpu
from jax.sharding import PartitionSpec as P

CHUNKS = 2
WIDE = 512
LANES = 128
GROUP = 8
TALL = 32
VMEM = 48 * 1024 * 1024
TALL_VMEM = 60 * 1024 * 1024


def tables(count):
    position = np.arange(count, dtype=np.int32)
    product = position[:, None] * position[None, :] % count
    angle = product.astype(np.float32) * np.float32(2.0 * math.pi / count)
    rounded = lambda value: value.astype(ml_dtypes.bfloat16).astype(np.float32)
    return (rounded(np.cos(angle)), rounded(np.sin(angle)))


def shifted(pieces, by):
    lane = lax.broadcasted_iota(jnp.int32, pieces[0].shape, 1)
    turned = [pltpu.roll(piece, by, 1) for piece in pieces]
    return jnp.concatenate(
        [jnp.where(lane < by, low, high) for low, high in zip(turned, turned[1:])], axis=1
    )


def shifted_back(pieces, by):
    lane = lax.broadcasted_iota(jnp.int32, pieces[0].shape, 1)
    turned = [pltpu.roll(piece, lax.rem(LANES - by, LANES), 1) for piece in pieces]
    return jnp.concatenate(
        [jnp.where(lane < LANES - by, low, high) for low, high in zip(turned, turned[1:])], axis=1
    )


def rolled_shots(offsets, counts, estimate, span, late):
    slots, rows, length = estimate.shape
    blocks = length // LANES
    for slot in range(slots):
        offset = offsets[slot]
        edge = offset // LANES
        pieces = []
        for j in range(span // LANES + 1):
            begin = lax.rem(blocks - 1 - edge + j, blocks) * LANES
            piece = estimate[slot, :, pl.ds(pl.multiple_of(begin, LANES), LANES)]
            wanted = (slot < counts[0]) & ((j <= edge) if late else (j > edge))
            pieces.append(jnp.where(wanted, piece, jnp.zeros_like(piece)))
        yield shifted(pieces, lax.rem(offset, LANES))


def tail_kernel(offsets, counts, estimate, *tails):
    total = sum(rolled_shots(offsets, counts, estimate, estimate.shape[2], True))
    piece = tails[0].shape[0]
    for chunk, tail in enumerate(tails):
        tail[...] = total[:, chunk * piece : (chunk + 1) * piece].T


def tails_of(estimate, offsets, counts):
    slots, width, length = estimate.shape
    piece = length // CHUNKS
    return pl.pallas_call(
        tail_kernel,
        grid_spec=pltpu.PrefetchScalarGridSpec(
            num_scalar_prefetch=2,
            grid=(width // width,),
            in_specs=[pl.BlockSpec((slots, width, length), lambda i, *_: (0, i, 0))],
            out_specs=[pl.BlockSpec((piece, width), lambda i, *_: (0, i))] * CHUNKS,
        ),
        out_shape=[jax.ShapeDtypeStruct((piece, width), jnp.bfloat16)] * CHUNKS,
        compiler_params=pltpu.CompilerParams(vmem_limit_bytes=TALL_VMEM),
        cost_estimate=pl.CostEstimate(
            flops=3_000_000_000, bytes_accessed=5_000_000, transcendentals=0
        ),
        name="tails",
    )(offsets, counts, estimate)


def lead_kernel(offsets, counts, estimate, observed, rest):
    total = observed[...].astype(jnp.float32)
    for moved in rolled_shots(offsets, counts, estimate, rest.shape[0], False):
        total = total - moved.astype(jnp.float32)
    rest[...] = total.T


def lead_of(estimate, observed, offsets, counts):
    slots, width, length = estimate.shape
    piece = length
    return pl.pallas_call(
        lead_kernel,
        grid_spec=pltpu.PrefetchScalarGridSpec(
            num_scalar_prefetch=2,
            grid=(width // width,),
            in_specs=[
                pl.BlockSpec((slots, width, length), lambda i, *_: (0, i, 0)),
                pl.BlockSpec((width, piece), lambda i, *_: (i, 0)),
            ],
            out_specs=pl.BlockSpec((piece, width), lambda i, *_: (0, i)),
        ),
        out_shape=jax.ShapeDtypeStruct((piece, width), jnp.float32),
        compiler_params=pltpu.CompilerParams(vmem_limit_bytes=VMEM),
        cost_estimate=pl.CostEstimate(
            flops=3_000_000_000, bytes_accessed=7_000_000, transcendentals=0
        ),
        name="lead",
    )(offsets, counts, estimate, observed)


def filter_kernel(scale, x, inward, ahead, behind, first, second, outward, y):
    lines, steps, width = x.shape
    half = inward.shape[1] // 2
    rows = lines * GROUP
    spec = jnp.dot(
        x[...].reshape(lines * steps, width), inward[...], preferred_element_type=jnp.float32
    ).reshape(lines, steps, 2 * half)
    w1, w2 = first[...], second[...]
    backs = []
    for at in range(0, steps, GROUP):
        part = spec[:, at : at + GROUP, :].reshape(rows, 2 * half).astype(jnp.bfloat16)
        both = jnp.dot(ahead[...], part, preferred_element_type=jnp.float32)
        weighted_re = w1 * both[:rows, :half] + w2 * both[rows:, half:]
        weighted_im = w2 * both[:rows, half:] - w1 * both[rows:, :half]
        weighted = jnp.concatenate([weighted_re, weighted_im], axis=0).astype(jnp.bfloat16)
        back = jnp.dot(behind[...], weighted, preferred_element_type=jnp.float32)
        backs.append(jnp.concatenate([back[:rows], back[rows:]], axis=1).astype(jnp.bfloat16))
    total = jnp.dot(
        jnp.concatenate(backs, axis=0), outward[...], preferred_element_type=jnp.float32
    )
    total = (total * scale).reshape(steps // GROUP, lines, GROUP, width)
    y[...] = jnp.concatenate(list(total), axis=1).astype(jnp.bfloat16)


def filter_tables(coherence):
    lines, width = coherence.shape
    half = width // 2
    padded = -(-half // LANES) * LANES
    cos_inline, sin_inline = tables(width)
    cos_cross, sin_cross = tables(lines)
    opposite = jnp.roll(coherence[::-1, ::-1], (1, 1), (0, 1))
    weight = 0.5 * (coherence + opposite)
    lowest = np.arange(half)[None, :] == 0
    first = weight[:, :half]
    second = jnp.where(lowest, weight[:, half : half + 1], first)

    def pad(value):
        return np.pad(value, ((0, 0), (0, padded - half)))

    def spread(value):
        return jnp.repeat(jnp.pad(value, ((0, 0), (0, padded - half))), GROUP, axis=0)

    def constant(value):
        return jnp.asarray(value.astype(ml_dtypes.bfloat16))

    cos_half = cos_inline[:, :half]
    im_half = np.where(lowest, cos_inline[:, half : half + 1], -sin_inline[:, :half])
    inward = np.concatenate([pad(cos_half), pad(im_half)], axis=1)
    double = np.where(lowest, 1.0, 2.0)
    outward = np.concatenate([pad(cos_half * double), pad(im_half * double)], axis=1).T
    unit = np.eye(GROUP)
    cos_wide = np.kron(cos_cross, unit)
    sin_wide = np.kron(sin_cross, unit)
    behind = np.block([[cos_wide, -sin_wide], [sin_wide, cos_wide]])
    return (
        constant(inward),
        constant(np.concatenate([cos_wide, sin_wide], axis=0)),
        constant(behind),
        spread(first),
        spread(second),
        constant(outward),
    )


def filtered(x, prepared, chunk, chunks):
    lines, width = x.shape[0], x.shape[2]
    steps = x.shape[1] // chunks
    scale = 1.0 / (lines * width)
    tall = min(TALL, steps)
    held = [
        pl.BlockSpec(value.shape, lambda i, r=value.ndim: (0,) * r) for value in prepared
    ]
    out = pl.pallas_call(
        functools.partial(filter_kernel, scale),
        grid=(steps // tall,),
        in_specs=[
            pl.BlockSpec((lines, tall, width), lambda i: (0, chunk * (steps // tall) + i, 0))
        ]
        + held,
        out_specs=pl.BlockSpec((lines, tall, width), lambda i: (0, i, 0)),
        out_shape=jax.ShapeDtypeStruct((lines, steps, width), jnp.bfloat16),
        compiler_params=pltpu.CompilerParams(vmem_limit_bytes=VMEM),
        cost_estimate=pl.CostEstimate(
            flops=steps * 120_000_000, bytes_accessed=4 * x.size, transcendentals=0
        ),
        name="filter",
    )(x, *prepared)
    return out.reshape(lines * steps, width)


def update_kernel(places, first, offsets, counts, base, *refs):
    *sources, out, turned, chosen = refs
    slots, width, tile = base.shape
    piece = sources[0].shape[0]
    span = turned.shape[1]
    window = tile + LANES
    low, high = places[0], places[-1] + piece
    step = first + pl.program_id(0)

    @pl.when(pl.program_id(0) == 0)
    def _():
        if low > 0:
            turned[:, pl.ds(low - window, window)] = jnp.zeros((width, window), jnp.bfloat16)
        if high < span:
            turned[:, pl.ds(high, window)] = jnp.zeros((width, window), jnp.bfloat16)
        for source, at in zip(sources, places):
            for row in range(0, piece, tile):
                turned[:, pl.ds(at + row, tile)] = source[pl.ds(row, tile), :].T
        row = lax.broadcasted_iota(jnp.int32, (window, tile), 0)
        column = lax.broadcasted_iota(jnp.int32, (window, tile), 1)
        for slot in range(slots):
            part = lax.rem(offsets[slot], LANES)
            chosen[slot] = (row == column + part).astype(jnp.float32).astype(jnp.bfloat16)

    for slot in range(slots):
        source_at = offsets[slot] + step * tile
        live = slot < counts[0]
        touched = live & (source_at + tile > low) & (source_at < high)

        @pl.when(touched)
        def _(slot=slot, source_at=source_at):
            begin = source_at // LANES
            taken = turned[:, pl.ds(pl.multiple_of(begin * LANES, LANES), window)]
            moved = jnp.dot(taken, chosen[slot], preferred_element_type=jnp.float32)
            out[slot] = (base[slot].astype(jnp.float32) + moved).astype(jnp.bfloat16)

        @pl.when(jnp.logical_not(touched))
        def _(slot=slot):
            out[slot] = jnp.where(live, base[slot], jnp.zeros_like(base[slot]))


def update(base, sources, offsets, counts, first, in_place):
    slots, width, length = base.shape
    places = tuple(sorted(sources))
    arrays = [sources[place] for place in places]
    piece = arrays[0].shape[0]
    tiles = length // WIDE - first
    spec = pl.BlockSpec((slots, width, WIDE), lambda i, *_: (0, 0, first + i))
    whole = pl.BlockSpec((piece, width), lambda i, *_: (0, 0))
    return pl.pallas_call(
        functools.partial(update_kernel, places, first),
        grid_spec=pltpu.PrefetchScalarGridSpec(
            num_scalar_prefetch=2,
            grid=(tiles,),
            in_specs=[spec] + [whole] * len(arrays),
            out_specs=spec,
            scratch_shapes=[
                pltpu.VMEM((width, 2 * length), jnp.bfloat16),
                pltpu.VMEM((slots, WIDE + LANES, WIDE), jnp.bfloat16),
            ],
        ),
        out_shape=jax.ShapeDtypeStruct((slots, width, length), jnp.bfloat16),
        input_output_aliases={2: 0} if in_place else {},
        compiler_params=pltpu.CompilerParams(vmem_limit_bytes=VMEM),
        cost_estimate=pl.CostEstimate(
            flops=2_000_000_000, bytes_accessed=9_000_000, transcendentals=0
        ),
        name="update",
    )(offsets, counts, base, *arrays)


def finish_kernel(offsets, counts, base, last, out, turned):
    slots, rows, size = base.shape
    piece = last.shape[0]
    blank = turned.shape[1] - piece
    at = pl.program_id(0) * size

    @pl.when(pl.program_id(0) == 0)
    def _():
        turned[:, :blank] = jnp.zeros((rows, blank), jnp.bfloat16)
        turned[:, blank:] = last[...].T

    for slot in range(slots):
        begin = (jnp.maximum(offsets[slot] - piece, 0) + at) // LANES
        pieces = [
            turned[:, pl.ds(pl.multiple_of((begin + j) * LANES, LANES), LANES)]
            for j in range(size // LANES + 1)
        ]
        moved = shifted_back(pieces, lax.rem(offsets[slot], LANES)).astype(jnp.float32)
        live = slot < counts[0]
        mine = live & (offsets[slot] > piece)
        total = base[slot].astype(jnp.float32) + jnp.where(mine, moved, 0.0)
        out[slot] = jnp.where(live, total, 0.0).astype(jnp.bfloat16)


def finish(base, last, offsets, counts):
    slots, width, length = base.shape
    piece = last.shape[0]
    size = piece // 2
    first = (length - piece) // size
    spec = pl.BlockSpec((slots, width, size), lambda i, *_: (0, 0, first + i))
    return pl.pallas_call(
        finish_kernel,
        grid_spec=pltpu.PrefetchScalarGridSpec(
            num_scalar_prefetch=2,
            grid=(piece // size,),
            in_specs=[spec, pl.BlockSpec((piece, width), lambda i, *_: (0, 0))],
            out_specs=spec,
            scratch_shapes=[pltpu.VMEM((width, 2 * piece), jnp.bfloat16)],
        ),
        out_shape=jax.ShapeDtypeStruct((slots, width, length), jnp.bfloat16),
        input_output_aliases={2: 0},
        compiler_params=pltpu.CompilerParams(vmem_limit_bytes=VMEM),
        cost_estimate=pl.CostEstimate(
            flops=10_000_000, bytes_accessed=4_000_000, transcendentals=0
        ),
        name="finish",
    )(offsets, counts, base, last)


def body(estimate, observed, offsets, counts, coherence):
    slots, _, width, length = estimate.shape
    lines = lax.axis_size("line")
    blocks = lax.axis_size("block")
    odd = lax.axis_index("block") % 2 == 1
    swaps = [(i, i ^ 1) for i in range(blocks)]
    hops = [(i, i + 2) for i in range(0, blocks - 2, 2)]
    back_by_one = [(i + 1, i) for i in range(blocks - 1)]
    estimate = estimate.reshape(slots, width, length)
    observed = observed.reshape(width, length)
    prepared = filter_tables(coherence)
    tails = tails_of(estimate, offsets, counts)
    swapped = [lax.ppermute(tail, "block", swaps) for tail in tails]
    crossed = [lax.ppermute(tail, "block", hops) for tail in swapped]
    rest = lead_of(estimate, observed, offsets, counts)
    incoming = jnp.concatenate(
        [jnp.where(odd, beside, before) for beside, before in zip(swapped, crossed)], axis=0
    )
    residual = (rest - incoming.astype(jnp.float32)).astype(jnp.bfloat16)
    residual = residual.reshape(lines, -1, width)
    spread = lax.all_to_all(residual, "line", split_axis=0, concat_axis=0, tiled=True)
    own = filtered(spread, prepared, 0, 1)
    own = lax.all_to_all(own, "line", split_axis=0, concat_axis=0, tiled=True)
    piece = length // CHUNKS
    own = [own[chunk * piece : (chunk + 1) * piece] for chunk in range(CHUNKS)]
    following = [lax.ppermute(part, "block", back_by_one) for part in own]
    sources = {at * piece: part for at, part in enumerate(own + following[:-1])}
    updated = update(estimate, sources, offsets, counts, 0, False)
    updated = finish(updated, following[-1], offsets, counts)
    return updated.reshape(slots, 1, width, length)


def solution(mesh):
    return jax.shard_map(
        body,
        mesh=mesh,
        in_specs=(
            P("block", "line", None, None),
            P("line", None, "block"),
            P("block"),
            P("block"),
            P(),
        ),
        out_specs=P("block", "line", None, None),
        check_vma=False,
    )
```

```python
import functools
import math

import jax
import jax.numpy as jnp
import ml_dtypes
import numpy as np
from jax import lax
from jax.experimental import pallas as pl
from jax.experimental.pallas import tpu as pltpu
from jax.sharding import PartitionSpec as P

CHUNKS = 2
WIDE = 512
LANES = 128
GROUP = 8
TALL = 32
VMEM = 48 * 1024 * 1024
TALL_VMEM = 60 * 1024 * 1024


def tables(count):
    position = np.arange(count, dtype=np.int32)
    product = position[:, None] * position[None, :] % count
    angle = product.astype(np.float32) * np.float32(2.0 * math.pi / count)
    rounded = lambda value: value.astype(ml_dtypes.bfloat16).astype(np.float32)
    return (rounded(np.cos(angle)), rounded(np.sin(angle)))


def shifted(pieces, by):
    lane = lax.broadcasted_iota(jnp.int32, pieces[0].shape, 1)
    turned = [pltpu.roll(piece, by, 1) for piece in pieces]
    return jnp.concatenate(
        [jnp.where(lane < by, low, high) for low, high in zip(turned, turned[1:])], axis=1
    )


def shifted_back(pieces, by):
    lane = lax.broadcasted_iota(jnp.int32, pieces[0].shape, 1)
    turned = [pltpu.roll(piece, lax.rem(LANES - by, LANES), 1) for piece in pieces]
    return jnp.concatenate(
        [jnp.where(lane < LANES - by, low, high) for low, high in zip(turned, turned[1:])], axis=1
    )


def rolled_shots(offsets, counts, estimate, span, late):
    slots, rows, length = estimate.shape
    blocks = length // LANES
    for slot in range(slots):
        offset = offsets[slot]
        edge = offset // LANES
        pieces = []
        for j in range(span // LANES + 1):
            begin = lax.rem(blocks - 1 - edge + j, blocks) * LANES
            piece = estimate[slot, :, pl.ds(pl.multiple_of(begin, LANES), LANES)]
            wanted = (slot < counts[0]) & ((j <= edge) if late else (j > edge))
            pieces.append(jnp.where(wanted, piece, jnp.zeros_like(piece)))
        yield shifted(pieces, lax.rem(offset, LANES))


def tail_kernel(offsets, counts, estimate, *tails):
    total = sum(rolled_shots(offsets, counts, estimate, estimate.shape[2], True))
    piece = tails[0].shape[0]
    for chunk, tail in enumerate(tails):
        tail[...] = total[:, chunk * piece : (chunk + 1) * piece].T


def tails_of(estimate, offsets, counts):
    slots, width, length = estimate.shape
    piece = length // CHUNKS
    return pl.pallas_call(
        tail_kernel,
        grid_spec=pltpu.PrefetchScalarGridSpec(
            num_scalar_prefetch=2,
            grid=(width // width,),
            in_specs=[pl.BlockSpec((slots, width, length), lambda i, *_: (0, i, 0))],
            out_specs=[pl.BlockSpec((piece, width), lambda i, *_: (0, i))] * CHUNKS,
        ),
        out_shape=[jax.ShapeDtypeStruct((piece, width), jnp.bfloat16)] * CHUNKS,
        compiler_params=pltpu.CompilerParams(vmem_limit_bytes=TALL_VMEM),
        cost_estimate=pl.CostEstimate(
            flops=3_000_000_000, bytes_accessed=5_000_000, transcendentals=0
        ),
        name="tails",
    )(offsets, counts, estimate)


def lead_kernel(offsets, counts, odd, estimate, observed, *refs):
    *swapped, rest = refs
    total = observed[...].astype(jnp.float32)
    for moved in rolled_shots(offsets, counts, estimate, rest.shape[0], False):
        total = total - moved.astype(jnp.float32)
    total = total.T
    piece = swapped[0].shape[0]
    for chunk, tail in enumerate(swapped):
        part = slice(chunk * piece, (chunk + 1) * piece)
        beside = jnp.where(odd[0] == 1, tail[...].astype(jnp.float32), 0.0)
        rest[part, :] = total[part] - beside


def lead_of(estimate, observed, offsets, counts, odd, swapped):
    slots, width, length = estimate.shape
    piece = swapped[0].shape[0]
    rows = pl.BlockSpec((piece, width), lambda i, *_: (0, i))
    return pl.pallas_call(
        lead_kernel,
        grid_spec=pltpu.PrefetchScalarGridSpec(
            num_scalar_prefetch=3,
            grid=(1,),
            in_specs=[
                pl.BlockSpec((slots, width, length), lambda i, *_: (0, i, 0)),
                pl.BlockSpec((width, length), lambda i, *_: (i, 0)),
            ]
            + [rows] * len(swapped),
            out_specs=pl.BlockSpec((length, width), lambda i, *_: (0, i)),
        ),
        out_shape=jax.ShapeDtypeStruct((length, width), jnp.float32),
        compiler_params=pltpu.CompilerParams(vmem_limit_bytes=VMEM),
        cost_estimate=pl.CostEstimate(
            flops=3_000_000_000, bytes_accessed=7_000_000, transcendentals=0
        ),
        name="lead",
    )(offsets, counts, odd, estimate, observed, *swapped)


def filter_kernel(scale, x, inward, ahead, behind, first, second, outward, y):
    lines, steps, width = x.shape
    half = inward.shape[1] // 2
    rows = lines * GROUP
    spec = jnp.dot(
        x[...].reshape(lines * steps, width), inward[...], preferred_element_type=jnp.float32
    ).reshape(lines, steps, 2 * half)
    w1, w2 = first[...], second[...]
    backs = []
    for at in range(0, steps, GROUP):
        part = spec[:, at : at + GROUP, :].reshape(rows, 2 * half).astype(jnp.bfloat16)
        both = jnp.dot(ahead[...], part, preferred_element_type=jnp.float32)
        weighted_re = w1 * both[:rows, :half] + w2 * both[rows:, half:]
        weighted_im = w2 * both[:rows, half:] - w1 * both[rows:, :half]
        weighted = jnp.concatenate([weighted_re, weighted_im], axis=0).astype(jnp.bfloat16)
        back = jnp.dot(behind[...], weighted, preferred_element_type=jnp.float32)
        backs.append(jnp.concatenate([back[:rows], back[rows:]], axis=1).astype(jnp.bfloat16))
    total = jnp.dot(
        jnp.concatenate(backs, axis=0), outward[...], preferred_element_type=jnp.float32
    )
    total = (total * scale).reshape(steps // GROUP, lines, GROUP, width)
    y[...] = jnp.concatenate(list(total), axis=1).astype(jnp.bfloat16)


def filter_tables(coherence):
    lines, width = coherence.shape
    half = width // 2
    padded = -(-half // LANES) * LANES
    cos_inline, sin_inline = tables(width)
    cos_cross, sin_cross = tables(lines)
    opposite = jnp.roll(coherence[::-1, ::-1], (1, 1), (0, 1))
    weight = 0.5 * (coherence + opposite)
    lowest = np.arange(half)[None, :] == 0
    first = weight[:, :half]
    second = jnp.where(lowest, weight[:, half : half + 1], first)

    def pad(value):
        return np.pad(value, ((0, 0), (0, padded - half)))

    def spread(value):
        return jnp.repeat(jnp.pad(value, ((0, 0), (0, padded - half))), GROUP, axis=0)

    def constant(value):
        return jnp.asarray(value.astype(ml_dtypes.bfloat16))

    cos_half = cos_inline[:, :half]
    im_half = np.where(lowest, cos_inline[:, half : half + 1], -sin_inline[:, :half])
    inward = np.concatenate([pad(cos_half), pad(im_half)], axis=1)
    double = np.where(lowest, 1.0, 2.0)
    outward = np.concatenate([pad(cos_half * double), pad(im_half * double)], axis=1).T
    unit = np.eye(GROUP)
    cos_wide = np.kron(cos_cross, unit)
    sin_wide = np.kron(sin_cross, unit)
    behind = np.block([[cos_wide, -sin_wide], [sin_wide, cos_wide]])
    return (
        constant(inward),
        constant(np.concatenate([cos_wide, sin_wide], axis=0)),
        constant(behind),
        spread(first),
        spread(second),
        constant(outward),
    )


def filtered(x, prepared, chunk, chunks):
    lines, width = x.shape[0], x.shape[2]
    steps = x.shape[1] // chunks
    scale = 1.0 / (lines * width)
    tall = min(TALL, steps)
    held = [
        pl.BlockSpec(value.shape, lambda i, r=value.ndim: (0,) * r) for value in prepared
    ]
    out = pl.pallas_call(
        functools.partial(filter_kernel, scale),
        grid=(steps // tall,),
        in_specs=[
            pl.BlockSpec((lines, tall, width), lambda i: (0, chunk * (steps // tall) + i, 0))
        ]
        + held,
        out_specs=pl.BlockSpec((lines, tall, width), lambda i: (0, i, 0)),
        out_shape=jax.ShapeDtypeStruct((lines, steps, width), jnp.bfloat16),
        compiler_params=pltpu.CompilerParams(vmem_limit_bytes=VMEM),
        cost_estimate=pl.CostEstimate(
            flops=steps * 120_000_000, bytes_accessed=4 * x.size, transcendentals=0
        ),
        name="filter",
    )(x, *prepared)
    return out.reshape(lines * steps, width)


def update_kernel(places, first, offsets, counts, base, *refs):
    *sources, out, turned, chosen = refs
    slots, width, tile = base.shape
    piece = sources[0].shape[0]
    span = turned.shape[1]
    window = tile + LANES
    low, high = places[0], places[-1] + piece
    step = first + pl.program_id(0)

    @pl.when(pl.program_id(0) == 0)
    def _():
        if low > 0:
            turned[:, pl.ds(low - window, window)] = jnp.zeros((width, window), jnp.bfloat16)
        if high < span:
            turned[:, pl.ds(high, window)] = jnp.zeros((width, window), jnp.bfloat16)
        for source, at in zip(sources, places):
            for row in range(0, piece, tile):
                turned[:, pl.ds(at + row, tile)] = source[pl.ds(row, tile), :].T
        row = lax.broadcasted_iota(jnp.int32, (window, tile), 0)
        column = lax.broadcasted_iota(jnp.int32, (window, tile), 1)
        for slot in range(slots):
            part = lax.rem(offsets[slot], LANES)
            chosen[slot] = (row == column + part).astype(jnp.float32).astype(jnp.bfloat16)

    for slot in range(slots):
        source_at = offsets[slot] + step * tile
        live = slot < counts[0]
        touched = live & (source_at + tile > low) & (source_at < high)

        @pl.when(touched)
        def _(slot=slot, source_at=source_at):
            begin = source_at // LANES
            taken = turned[:, pl.ds(pl.multiple_of(begin * LANES, LANES), window)]
            moved = jnp.dot(taken, chosen[slot], preferred_element_type=jnp.float32)
            out[slot] = (base[slot].astype(jnp.float32) + moved).astype(jnp.bfloat16)

        @pl.when(jnp.logical_not(touched))
        def _(slot=slot):
            out[slot] = jnp.where(live, base[slot], jnp.zeros_like(base[slot]))


def update(base, sources, offsets, counts, first, in_place):
    slots, width, length = base.shape
    places = tuple(sorted(sources))
    arrays = [sources[place] for place in places]
    piece = arrays[0].shape[0]
    tiles = length // WIDE - first
    spec = pl.BlockSpec((slots, width, WIDE), lambda i, *_: (0, 0, first + i))
    whole = pl.BlockSpec((piece, width), lambda i, *_: (0, 0))
    return pl.pallas_call(
        functools.partial(update_kernel, places, first),
        grid_spec=pltpu.PrefetchScalarGridSpec(
            num_scalar_prefetch=2,
            grid=(tiles,),
            in_specs=[spec] + [whole] * len(arrays),
            out_specs=spec,
            scratch_shapes=[
                pltpu.VMEM((width, 2 * length), jnp.bfloat16),
                pltpu.VMEM((slots, WIDE + LANES, WIDE), jnp.bfloat16),
            ],
        ),
        out_shape=jax.ShapeDtypeStruct((slots, width, length), jnp.bfloat16),
        input_output_aliases={2: 0} if in_place else {},
        compiler_params=pltpu.CompilerParams(vmem_limit_bytes=VMEM),
        cost_estimate=pl.CostEstimate(
            flops=2_000_000_000, bytes_accessed=9_000_000, transcendentals=0
        ),
        name="update",
    )(offsets, counts, base, *arrays)


def finish_kernel(offsets, counts, base, last, out, turned):
    slots, rows, size = base.shape
    piece = last.shape[0]
    blank = turned.shape[1] - piece
    at = pl.program_id(0) * size

    @pl.when(pl.program_id(0) == 0)
    def _():
        turned[:, :blank] = jnp.zeros((rows, blank), jnp.bfloat16)
        turned[:, blank:] = last[...].T

    for slot in range(slots):
        begin = (jnp.maximum(offsets[slot] - piece, 0) + at) // LANES
        pieces = [
            turned[:, pl.ds(pl.multiple_of((begin + j) * LANES, LANES), LANES)]
            for j in range(size // LANES + 1)
        ]
        moved = shifted_back(pieces, lax.rem(offsets[slot], LANES)).astype(jnp.float32)
        live = slot < counts[0]
        mine = live & (offsets[slot] > piece)
        total = base[slot].astype(jnp.float32) + jnp.where(mine, moved, 0.0)
        out[slot] = jnp.where(live, total, 0.0).astype(jnp.bfloat16)


def finish(base, last, offsets, counts):
    slots, width, length = base.shape
    piece = last.shape[0]
    size = piece // 2
    first = (length - piece) // size
    spec = pl.BlockSpec((slots, width, size), lambda i, *_: (0, 0, first + i))
    return pl.pallas_call(
        finish_kernel,
        grid_spec=pltpu.PrefetchScalarGridSpec(
            num_scalar_prefetch=2,
            grid=(piece // size,),
            in_specs=[spec, pl.BlockSpec((piece, width), lambda i, *_: (0, 0))],
            out_specs=spec,
            scratch_shapes=[pltpu.VMEM((width, 2 * piece), jnp.bfloat16)],
        ),
        out_shape=jax.ShapeDtypeStruct((slots, width, length), jnp.bfloat16),
        input_output_aliases={2: 0},
        compiler_params=pltpu.CompilerParams(vmem_limit_bytes=VMEM),
        cost_estimate=pl.CostEstimate(
            flops=10_000_000, bytes_accessed=4_000_000, transcendentals=0
        ),
        name="finish",
    )(offsets, counts, base, last)


def body(estimate, observed, offsets, counts, coherence):
    slots, _, width, length = estimate.shape
    lines = lax.axis_size("line")
    blocks = lax.axis_size("block")
    odd = (lax.axis_index("block") % 2).astype(jnp.int32).reshape(1)
    swaps = [(i, i ^ 1) for i in range(blocks)]
    hops = [(i, i + 2) for i in range(0, blocks - 2, 2)]
    back_by_one = [(i + 1, i) for i in range(blocks - 1)]
    estimate = estimate.reshape(slots, width, length)
    observed = observed.reshape(width, length)
    prepared = filter_tables(coherence)
    tails = tails_of(estimate, offsets, counts)
    swapped = [lax.ppermute(tail, "block", swaps) for tail in tails]
    crossed = [lax.ppermute(tail, "block", hops) for tail in swapped]
    rest = lead_of(estimate, observed, offsets, counts, odd, swapped)
    incoming = jnp.concatenate(crossed, axis=0)
    residual = (rest - incoming.astype(jnp.float32)).astype(jnp.bfloat16)
    residual = residual.reshape(lines, -1, width)
    spread = lax.all_to_all(residual, "line", split_axis=0, concat_axis=0, tiled=True)
    own = filtered(spread, prepared, 0, 1)
    own = lax.all_to_all(own, "line", split_axis=0, concat_axis=0, tiled=True)
    piece = length // CHUNKS
    own = [own[chunk * piece : (chunk + 1) * piece] for chunk in range(CHUNKS)]
    following = [lax.ppermute(part, "block", back_by_one) for part in own]
    sources = {at * piece: part for at, part in enumerate(own + following[:-1])}
    updated = update(estimate, sources, offsets, counts, 0, False)
    updated = finish(updated, following[-1], offsets, counts)
    return updated.reshape(slots, 1, width, length)


def solution(mesh):
    return jax.shard_map(
        body,
        mesh=mesh,
        in_specs=(
            P("block", "line", None, None),
            P("line", None, "block"),
            P("block"),
            P("block"),
            P(),
        ),
        out_specs=P("block", "line", None, None),
        check_vma=False,
    )
```

```python
import functools
import math

import jax
import jax.numpy as jnp
import ml_dtypes
import numpy as np
from jax import lax
from jax.experimental import pallas as pl
from jax.experimental.pallas import tpu as pltpu
from jax.sharding import PartitionSpec as P

CHUNKS = 2
WIDE = 512
LANES = 128
GROUP = 8
TALL = 64
VMEM = 48 * 1024 * 1024
TALL_VMEM = 60 * 1024 * 1024


def tables(count):
    position = np.arange(count, dtype=np.int32)
    product = position[:, None] * position[None, :] % count
    angle = product.astype(np.float32) * np.float32(2.0 * math.pi / count)
    rounded = lambda value: value.astype(ml_dtypes.bfloat16).astype(np.float32)
    return (rounded(np.cos(angle)), rounded(np.sin(angle)))


def shifted(pieces, by):
    lane = lax.broadcasted_iota(jnp.int32, pieces[0].shape, 1)
    turned = [pltpu.roll(piece, by, 1) for piece in pieces]
    return jnp.concatenate(
        [jnp.where(lane < by, low, high) for low, high in zip(turned, turned[1:])], axis=1
    )


def shifted_back(pieces, by):
    lane = lax.broadcasted_iota(jnp.int32, pieces[0].shape, 1)
    turned = [pltpu.roll(piece, lax.rem(LANES - by, LANES), 1) for piece in pieces]
    return jnp.concatenate(
        [jnp.where(lane < LANES - by, low, high) for low, high in zip(turned, turned[1:])], axis=1
    )


def rolled_shots(offsets, counts, estimate, span, late):
    slots, rows, length = estimate.shape
    blocks = length // LANES
    for slot in range(slots):
        offset = offsets[slot]
        edge = offset // LANES
        pieces = []
        for j in range(span // LANES + 1):
            begin = lax.rem(blocks - 1 - edge + j, blocks) * LANES
            piece = estimate[slot, :, pl.ds(pl.multiple_of(begin, LANES), LANES)]
            wanted = (slot < counts[0]) & ((j <= edge) if late else (j > edge))
            pieces.append(jnp.where(wanted, piece, jnp.zeros_like(piece)))
        yield shifted(pieces, lax.rem(offset, LANES))


def tail_kernel(offsets, counts, estimate, *tails):
    total = sum(rolled_shots(offsets, counts, estimate, estimate.shape[2], True))
    piece = tails[0].shape[0]
    for chunk, tail in enumerate(tails):
        tail[...] = total[:, chunk * piece : (chunk + 1) * piece].T


def tails_of(estimate, offsets, counts):
    slots, width, length = estimate.shape
    piece = length // CHUNKS
    return pl.pallas_call(
        tail_kernel,
        grid_spec=pltpu.PrefetchScalarGridSpec(
            num_scalar_prefetch=2,
            grid=(width // width,),
            in_specs=[pl.BlockSpec((slots, width, length), lambda i, *_: (0, i, 0))],
            out_specs=[pl.BlockSpec((piece, width), lambda i, *_: (0, i))] * CHUNKS,
        ),
        out_shape=[jax.ShapeDtypeStruct((piece, width), jnp.bfloat16)] * CHUNKS,
        compiler_params=pltpu.CompilerParams(vmem_limit_bytes=TALL_VMEM),
        cost_estimate=pl.CostEstimate(
            flops=3_000_000_000, bytes_accessed=5_000_000, transcendentals=0
        ),
        name="tails",
    )(offsets, counts, estimate)


def lead_kernel(offsets, counts, estimate, observed, rest):
    total = observed[...].astype(jnp.float32)
    for moved in rolled_shots(offsets, counts, estimate, rest.shape[0], False):
        total = total - moved.astype(jnp.float32)
    rest[...] = total.T


def lead_of(estimate, observed, offsets, counts):
    slots, width, length = estimate.shape
    piece = length
    return pl.pallas_call(
        lead_kernel,
        grid_spec=pltpu.PrefetchScalarGridSpec(
            num_scalar_prefetch=2,
            grid=(width // width,),
            in_specs=[
                pl.BlockSpec((slots, width, length), lambda i, *_: (0, i, 0)),
                pl.BlockSpec((width, piece), lambda i, *_: (i, 0)),
            ],
            out_specs=pl.BlockSpec((piece, width), lambda i, *_: (0, i)),
        ),
        out_shape=jax.ShapeDtypeStruct((piece, width), jnp.float32),
        compiler_params=pltpu.CompilerParams(vmem_limit_bytes=VMEM),
        cost_estimate=pl.CostEstimate(
            flops=3_000_000_000, bytes_accessed=7_000_000, transcendentals=0
        ),
        name="lead",
    )(offsets, counts, estimate, observed)


def filter_kernel(scale, x, inward, ahead, behind, first, second, outward, y):
    lines, steps, width = x.shape
    half = inward.shape[1] // 2
    rows = lines * GROUP
    spec = jnp.dot(
        x[...].reshape(lines * steps, width), inward[...], preferred_element_type=jnp.float32
    ).reshape(lines, steps, 2 * half)
    w1, w2 = first[...], second[...]
    backs = []
    for at in range(0, steps, GROUP):
        part = spec[:, at : at + GROUP, :].reshape(rows, 2 * half).astype(jnp.bfloat16)
        both = jnp.dot(ahead[...], part, preferred_element_type=jnp.float32)
        weighted_re = w1 * both[:rows, :half] + w2 * both[rows:, half:]
        weighted_im = w2 * both[:rows, half:] - w1 * both[rows:, :half]
        weighted = jnp.concatenate([weighted_re, weighted_im], axis=0).astype(jnp.bfloat16)
        back = jnp.dot(behind[...], weighted, preferred_element_type=jnp.float32)
        backs.append(jnp.concatenate([back[:rows], back[rows:]], axis=1).astype(jnp.bfloat16))
    total = jnp.dot(
        jnp.concatenate(backs, axis=0), outward[...], preferred_element_type=jnp.float32
    )
    total = (total * scale).reshape(steps // GROUP, lines, GROUP, width)
    y[...] = jnp.concatenate(list(total), axis=1).astype(jnp.bfloat16)


def filter_tables(coherence):
    lines, width = coherence.shape
    half = width // 2
    padded = -(-half // LANES) * LANES
    cos_inline, sin_inline = tables(width)
    cos_cross, sin_cross = tables(lines)
    opposite = jnp.roll(coherence[::-1, ::-1], (1, 1), (0, 1))
    weight = 0.5 * (coherence + opposite)
    lowest = np.arange(half)[None, :] == 0
    first = weight[:, :half]
    second = jnp.where(lowest, weight[:, half : half + 1], first)

    def pad(value):
        return np.pad(value, ((0, 0), (0, padded - half)))

    def spread(value):
        return jnp.repeat(jnp.pad(value, ((0, 0), (0, padded - half))), GROUP, axis=0)

    def constant(value):
        return jnp.asarray(value.astype(ml_dtypes.bfloat16))

    cos_half = cos_inline[:, :half]
    im_half = np.where(lowest, cos_inline[:, half : half + 1], -sin_inline[:, :half])
    inward = np.concatenate([pad(cos_half), pad(im_half)], axis=1)
    double = np.where(lowest, 1.0, 2.0)
    outward = np.concatenate([pad(cos_half * double), pad(im_half * double)], axis=1).T
    unit = np.eye(GROUP)
    cos_wide = np.kron(cos_cross, unit)
    sin_wide = np.kron(sin_cross, unit)
    behind = np.block([[cos_wide, -sin_wide], [sin_wide, cos_wide]])
    return (
        constant(inward),
        constant(np.concatenate([cos_wide, sin_wide], axis=0)),
        constant(behind),
        spread(first),
        spread(second),
        constant(outward),
    )


def filtered(x, prepared, chunk, chunks):
    lines, width = x.shape[0], x.shape[2]
    steps = x.shape[1] // chunks
    scale = 1.0 / (lines * width)
    tall = min(TALL, steps)
    held = [
        pl.BlockSpec(value.shape, lambda i, r=value.ndim: (0,) * r) for value in prepared
    ]
    out = pl.pallas_call(
        functools.partial(filter_kernel, scale),
        grid=(steps // tall,),
        in_specs=[
            pl.BlockSpec((lines, tall, width), lambda i: (0, chunk * (steps // tall) + i, 0))
        ]
        + held,
        out_specs=pl.BlockSpec((lines, tall, width), lambda i: (0, i, 0)),
        out_shape=jax.ShapeDtypeStruct((lines, steps, width), jnp.bfloat16),
        compiler_params=pltpu.CompilerParams(vmem_limit_bytes=VMEM),
        cost_estimate=pl.CostEstimate(
            flops=steps * 120_000_000, bytes_accessed=4 * x.size, transcendentals=0
        ),
        name="filter",
    )(x, *prepared)
    return out.reshape(lines * steps, width)


def update_kernel(places, first, offsets, counts, base, *refs):
    *sources, out, turned, chosen = refs
    slots, width, tile = base.shape
    piece = sources[0].shape[0]
    span = turned.shape[1]
    window = tile + LANES
    low, high = places[0], places[-1] + piece
    step = first + pl.program_id(0)

    @pl.when(pl.program_id(0) == 0)
    def _():
        if low > 0:
            turned[:, pl.ds(low - window, window)] = jnp.zeros((width, window), jnp.bfloat16)
        if high < span:
            turned[:, pl.ds(high, window)] = jnp.zeros((width, window), jnp.bfloat16)
        for source, at in zip(sources, places):
            for row in range(0, piece, tile):
                turned[:, pl.ds(at + row, tile)] = source[pl.ds(row, tile), :].T
        row = lax.broadcasted_iota(jnp.int32, (window, tile), 0)
        column = lax.broadcasted_iota(jnp.int32, (window, tile), 1)
        for slot in range(slots):
            part = lax.rem(offsets[slot], LANES)
            chosen[slot] = (row == column + part).astype(jnp.float32).astype(jnp.bfloat16)

    for slot in range(slots):
        source_at = offsets[slot] + step * tile
        live = slot < counts[0]
        touched = live & (source_at + tile > low) & (source_at < high)

        @pl.when(touched)
        def _(slot=slot, source_at=source_at):
            begin = source_at // LANES
            taken = turned[:, pl.ds(pl.multiple_of(begin * LANES, LANES), window)]
            moved = jnp.dot(taken, chosen[slot], preferred_element_type=jnp.float32)
            out[slot] = (base[slot].astype(jnp.float32) + moved).astype(jnp.bfloat16)

        @pl.when(jnp.logical_not(touched))
        def _(slot=slot):
            out[slot] = jnp.where(live, base[slot], jnp.zeros_like(base[slot]))


def update(base, sources, offsets, counts, first, in_place):
    slots, width, length = base.shape
    places = tuple(sorted(sources))
    arrays = [sources[place] for place in places]
    piece = arrays[0].shape[0]
    tiles = length // WIDE - first
    spec = pl.BlockSpec((slots, width, WIDE), lambda i, *_: (0, 0, first + i))
    whole = pl.BlockSpec((piece, width), lambda i, *_: (0, 0))
    return pl.pallas_call(
        functools.partial(update_kernel, places, first),
        grid_spec=pltpu.PrefetchScalarGridSpec(
            num_scalar_prefetch=2,
            grid=(tiles,),
            in_specs=[spec] + [whole] * len(arrays),
            out_specs=spec,
            scratch_shapes=[
                pltpu.VMEM((width, 2 * length), jnp.bfloat16),
                pltpu.VMEM((slots, WIDE + LANES, WIDE), jnp.bfloat16),
            ],
        ),
        out_shape=jax.ShapeDtypeStruct((slots, width, length), jnp.bfloat16),
        input_output_aliases={2: 0} if in_place else {},
        compiler_params=pltpu.CompilerParams(vmem_limit_bytes=VMEM),
        cost_estimate=pl.CostEstimate(
            flops=2_000_000_000, bytes_accessed=9_000_000, transcendentals=0
        ),
        name="update",
    )(offsets, counts, base, *arrays)


def finish_kernel(offsets, counts, base, last, out, turned):
    slots, rows, size = base.shape
    piece = last.shape[0]
    blank = turned.shape[1] - piece
    at = pl.program_id(0) * size

    @pl.when(pl.program_id(0) == 0)
    def _():
        turned[:, :blank] = jnp.zeros((rows, blank), jnp.bfloat16)
        turned[:, blank:] = last[...].T

    for slot in range(slots):
        begin = (jnp.maximum(offsets[slot] - piece, 0) + at) // LANES
        pieces = [
            turned[:, pl.ds(pl.multiple_of((begin + j) * LANES, LANES), LANES)]
            for j in range(size // LANES + 1)
        ]
        moved = shifted_back(pieces, lax.rem(offsets[slot], LANES)).astype(jnp.float32)
        live = slot < counts[0]
        mine = live & (offsets[slot] > piece)
        total = base[slot].astype(jnp.float32) + jnp.where(mine, moved, 0.0)
        out[slot] = jnp.where(live, total, 0.0).astype(jnp.bfloat16)


def finish(base, last, offsets, counts):
    slots, width, length = base.shape
    piece = last.shape[0]
    size = piece // 2
    first = (length - piece) // size
    spec = pl.BlockSpec((slots, width, size), lambda i, *_: (0, 0, first + i))
    return pl.pallas_call(
        finish_kernel,
        grid_spec=pltpu.PrefetchScalarGridSpec(
            num_scalar_prefetch=2,
            grid=(piece // size,),
            in_specs=[spec, pl.BlockSpec((piece, width), lambda i, *_: (0, 0))],
            out_specs=spec,
            scratch_shapes=[pltpu.VMEM((width, 2 * piece), jnp.bfloat16)],
        ),
        out_shape=jax.ShapeDtypeStruct((slots, width, length), jnp.bfloat16),
        input_output_aliases={2: 0},
        compiler_params=pltpu.CompilerParams(vmem_limit_bytes=VMEM),
        cost_estimate=pl.CostEstimate(
            flops=10_000_000, bytes_accessed=4_000_000, transcendentals=0
        ),
        name="finish",
    )(offsets, counts, base, last)


def body(estimate, observed, offsets, counts, coherence):
    slots, _, width, length = estimate.shape
    lines = lax.axis_size("line")
    blocks = lax.axis_size("block")
    odd = lax.axis_index("block") % 2 == 1
    swaps = [(i, i ^ 1) for i in range(blocks)]
    hops = [(i, i + 2) for i in range(0, blocks - 2, 2)]
    back_by_one = [(i + 1, i) for i in range(blocks - 1)]
    estimate = estimate.reshape(slots, width, length)
    observed = observed.reshape(width, length)
    prepared = filter_tables(coherence)
    tails = tails_of(estimate, offsets, counts)
    swapped = [lax.ppermute(tail, "block", swaps) for tail in tails]
    crossed = [lax.ppermute(tail, "block", hops) for tail in swapped]
    rest = lead_of(estimate, observed, offsets, counts)
    incoming = jnp.concatenate(
        [jnp.where(odd, beside, before) for beside, before in zip(swapped, crossed)], axis=0
    )
    residual = (rest - incoming.astype(jnp.float32)).astype(jnp.bfloat16)
    residual = residual.reshape(lines, -1, width)
    spread = lax.all_to_all(residual, "line", split_axis=0, concat_axis=0, tiled=True)
    own = filtered(spread, prepared, 0, 1)
    own = lax.all_to_all(own, "line", split_axis=0, concat_axis=0, tiled=True)
    piece = length // CHUNKS
    own = [own[chunk * piece : (chunk + 1) * piece] for chunk in range(CHUNKS)]
    following = [lax.ppermute(part, "block", back_by_one) for part in own]
    sources = {at * piece: part for at, part in enumerate(own + following[:-1])}
    updated = update(estimate, sources, offsets, counts, 0, False)
    updated = finish(updated, following[-1], offsets, counts)
    return updated.reshape(slots, 1, width, length)


def solution(mesh):
    return jax.shard_map(
        body,
        mesh=mesh,
        in_specs=(
            P("block", "line", None, None),
            P("line", None, "block"),
            P("block"),
            P("block"),
            P(),
        ),
        out_specs=P("block", "line", None, None),
        check_vma=False,
    )
```
